32 devices in a mesh: gr: 8 (over y, x, core), gc: 4 (over z).
Axes of the slice: x: 2, y: 2, z: 4, core: 2. Of those that a mesh axis runs over, the one named last changes fastest.
Arguments:
- x_states: bfloat16 [32768, 512], P(('gr', 'gc'))
- y_states: bfloat16 [32768, 512], P(('gr', 'gc')), as said below
Outputs:
- proj_x: bfloat16 [32768, 512], P(('gr', 'gc'))
- proj_y: bfloat16 [32768, 512], P(('gr', 'gc'))
- cross: float32 [512, 512], replicated
Inputs may be any that keep to these rules, and one draw needn't show every extreme that they name: `y_states`: paired with x_states row by row.
All inputs are finite; a program needn't handle non-finite values.
Results may differ from the reference program's by a relative error of at most 0.0015.
Values sent between devices are 32-bit elements; how exact they have to be, the bound alone decides.
No kernel may reach another device: no remote copies, remote signals or barrier semaphores. Data moves between devices by JAX's collectives and lax.ppermute only.
A program may use at most 64 MiB of HBM per device.

```python
import jax
import jax.numpy as jnp
from jax import lax

PW = 512
ROWS = 32768


def paired_states(key):
    base_key = jax.random.fold_in(key, 7001)
    k_one, k_two, k_three, k_four = jax.random.split(base_key, 4)
    source = jax.random.normal(k_one, (ROWS, PW), jnp.float32)
    noise = jax.random.normal(k_two, (ROWS, PW), jnp.float32)
    scale_x = jnp.exp(jax.random.uniform(k_three, (1, PW), jnp.float32, -1.2, 1.2))
    scale_y = jnp.exp(jax.random.uniform(k_four, (1, PW), jnp.float32, -1.2, 1.2))
    mixed = 0.5 * source + 0.4 * jnp.roll(source, 1, axis=1) + 0.3 * jnp.roll(source, -5, axis=1) + 0.3 * jnp.roll(source, 11, axis=1)
    x_full = source * scale_x
    y_full = (mixed + 0.6 * noise) * scale_y
    return (x_full, y_full)


def draw_x_states(key, part):
    return paired_states(key)[0].astype(jnp.bfloat16)


def draw_y_states(key, part):
    return paired_states(key)[1].astype(jnp.bfloat16)


def setup_inputs(seed: int = 0) -> dict:
    arg_keys = jax.random.split(jax.random.key(seed), 3)
    x_states = draw_x_states(jax.random.fold_in(arg_keys[2], 71), 0)
    y_states = draw_y_states(jax.random.fold_in(arg_keys[2], 71), 0)
    return {"x_states": x_states, "y_states": y_states}


RIDGE = 0.1

def reference(x_states, y_states):
    eye = jnp.eye(PW, dtype=jnp.float32)
    cov_x = jnp.dot(x_states.T.astype(jnp.float32), x_states.astype(jnp.float32), preferred_element_type=jnp.float32) / ROWS + RIDGE * eye
    cov_y = jnp.dot(y_states.T.astype(jnp.float32), y_states.astype(jnp.float32), preferred_element_type=jnp.float32) / ROWS + RIDGE * eye
    cov_xy = jnp.dot(x_states.T.astype(jnp.float32), y_states.astype(jnp.float32), preferred_element_type=jnp.float32) / ROWS
    low_x = jnp.linalg.cholesky(cov_x)
    low_y = jnp.linalg.cholesky(cov_y)
    left = jax.scipy.linalg.solve_triangular(low_x, cov_xy, lower=True)
    cross = jax.scipy.linalg.solve_triangular(low_y, left.T, lower=True).T
    white_x = jax.scipy.linalg.solve_triangular(low_x, x_states.astype(jnp.float32).T, lower=True).T
    white_y = jax.scipy.linalg.solve_triangular(low_y, y_states.astype(jnp.float32).T, lower=True).T
    proj_x = jnp.dot(white_x, cross, precision=lax.Precision.HIGHEST).astype(jnp.bfloat16)
    proj_y = jnp.dot(white_y, cross.T, precision=lax.Precision.HIGHEST).astype(jnp.bfloat16)
    return (proj_x, proj_y, cross)
```

```python
import jax
import jax.numpy as jnp
from jax import lax
from jax.experimental import pallas as pl
from jax.experimental.pallas import tpu as pltpu
from jax.sharding import PartitionSpec as P

RIDGE = 0.1
B = 128
NB = 16
BF = jnp.bfloat16
F32 = jnp.float32
VMEM_LIMIT = 48 * 1024 * 1024


def dot(a, b, ca=1, cb=0, precision=None):
    return lax.dot_general(a, b, (((ca,), (cb,)), ((), ())), preferred_element_type=F32, precision=precision)


def dot_f32(a, b, ca=1, cb=0):
    return dot(a, b, ca, cb, lax.Precision.HIGHEST)


def split2(a):
    high = a.astype(BF)
    return high, (a - high.astype(F32)).astype(BF)


def split3(a):
    high = a.astype(BF)
    rest = a - high.astype(F32)
    mid = rest.astype(BF)
    return high, mid, (rest - mid.astype(F32)).astype(BF)


def dot_x3(a, b, ca=1, cb=0):
    ah, al = a
    bh, bl = b
    return dot(ah, bh, ca, cb) + (dot(ah, bl, ca, cb) + dot(al, bh, ca, cb))


def outer_sum(u, v):
    uh, um, ul = split3(u)
    vh, vm, vl = split3(v)
    a = jnp.concatenate([uh, uh, um, uh, ul, um], 0)
    b = jnp.concatenate([vh, vm, vh, vl, vh, vm], 0)
    return dot(a, b, 0, 0)


def inverse_factor(a):
    n = a.shape[0]
    r = lax.broadcasted_iota(jnp.int32, (n, n), 0)
    c = lax.broadcasted_iota(jnp.int32, (n, n), 1)
    z = jnp.where(r == c, 1.0, 0.0).astype(F32)
    rows = lax.broadcasted_iota(jnp.int32, (NB, n), 0)
    out = []
    for s in range(n // NB):
        t, v = a[:NB], z[:NB]
        cols = [jnp.broadcast_to(t[:, NB * s + q : NB * s + q + 1], (NB, n)) for q in range(NB)]
        pivots = jnp.zeros((NB, n), F32)
        for k in range(NB):
            d = cols[k][k : k + 1, :]
            pivots = jnp.where(rows == k, d, pivots)
            if k == NB - 1:
                break
            m = jnp.where(rows > k, cols[k] * (1.0 / d), 0.0)
            t = t - m * t[k : k + 1, :]
            v = v - m * v[k : k + 1, :]
            for q in range(k + 1, NB):
                cols[q] = cols[q] - m * cols[q][k : k + 1, :]
        scale = lax.rsqrt(pivots)
        t, v = t * scale, v * scale
        out.append(v)
        if NB * (s + 1) < n:
            update = outer_sum(t[:, NB * (s + 1) :], jnp.concatenate([t, v], 1))
            a, z = a[NB:] - update[:, :n], z[NB:] - update[:, n:]
    return jnp.concatenate(out, 0)


def upper_blocks(n):
    return [(i, j) for i in range(n) for j in range(i, n)]


def lower_blocks(n):
    return [(i, j) for i in range(n) for j in range(i + 1)]


def gram_kernel(partner, core_ref, x_ref, y_ref, o_ref, a_ref):
    width = x_ref.shape[1]
    n = width // B
    core = core_ref[0]
    owner = 1 - core if partner else core

    @pl.when(owner == 0)
    def _():
        a_ref[...] = x_ref[...]

    @pl.when(owner == 1)
    def _():
        a_ref[...] = y_ref[...]

    row = 0
    for i in range(n):
        g = dot(a_ref[:, B * i : B * (i + 1)], a_ref[:, B * i :], 0, 0)
        for j in range(n - i):
            o_ref[row : row + B, :] = g[:, B * j : B * (j + 1)]
            row += B
    half = width // 2
    columns = pl.ds(pl.multiple_of(owner * half, half), half)
    g = dot(x_ref[...], y_ref[:, columns], 0, 0)
    for j in range(half // B):
        o_ref[row : row + width, :] = g[:, B * j : B * (j + 1)]
        row += width


def factor_kernel(total_rows, n, s_ref, o_ref, f_ref):
    r = lax.broadcasted_iota(jnp.int32, (B, B), 0)
    c = lax.broadcasted_iota(jnp.int32, (B, B), 1)
    ridge = jnp.where(r == c, RIDGE, 0.0).astype(F32)
    at = lambda i: slice(B * i, B * (i + 1))
    for k, (i, j) in enumerate(upper_blocks(n)):
        block = s_ref[at(k), :] / total_rows
        f_ref[at(i), at(j)] = block + ridge if i == j else block
    for b in range(n):
        w = inverse_factor(f_ref[at(b), at(b)])
        f_ref[at(b), at(b)] = w
        if b > 0:
            f_ref[at(b), : B * b] = dot_f32(w, f_ref[at(b), : B * b])
        if b < n - 1:
            f_ref[at(b), B * (b + 1) :] = dot_f32(w, f_ref[at(b), B * (b + 1) :])
        for i in range(b + 1, n):
            u = f_ref[at(b), at(i)]
            f_ref[at(i), B * i :] -= dot_f32(u, f_ref[at(b), B * i :], 0, 0)
            if b > 0:
                f_ref[at(i), : B * b] -= dot_f32(u, f_ref[at(b), : B * b], 0, 0)
            f_ref[at(i), at(b)] = -dot_f32(u, w, 0, 0)
    for k, (i, j) in enumerate(lower_blocks(n)):
        o_ref[at(k), :] = f_ref[at(i), at(j)]


def project_kernel(core_ref, x_ref, y_ref, wm_ref, wo_ref, cm_ref, co_ref, px_ref, py_ref, cross_ref, wx_ref, wy_ref, c_ref):
    width = x_ref.shape[1]
    n = width // B
    half = width // 2
    core = core_ref[0]
    at = lambda i: slice(B * i, B * (i + 1))

    def unpack(w_x, w_y, c_0, c_1):
        for k, (i, j) in enumerate(lower_blocks(n)):
            wx_ref[at(i), at(j)] = w_x[at(k), :]
            wy_ref[at(i), at(j)] = w_y[at(k), :]
        for j in range(half // B):
            c_ref[:, B * j : B * (j + 1)] = c_0[width * j : width * (j + 1), :]
            c_ref[:, half + B * j : half + B * (j + 1)] = c_1[width * j : width * (j + 1), :]

    @pl.when(core == 0)
    def _():
        unpack(wm_ref, wo_ref, cm_ref, co_ref)

    @pl.when(core == 1)
    def _():
        unpack(wo_ref, wm_ref, co_ref, cm_ref)

    c_hl = split2(c_ref[...])
    left = []
    for i in range(n):
        k = B * (i + 1)
        left.append(dot_x3(split2(wx_ref[at(i), :k]), [e[:k] for e in c_hl]))
    left = split2(jnp.concatenate(left, 0))
    for j in range(n):
        k = B * (j + 1)
        cross_ref[:, at(j)] = dot_x3([e[:, :k] for e in left], split2(wy_ref[at(j), :k]), 1, 1)
    cross = split2(cross_ref[...])
    map_x, map_y = [], []
    for i in range(n):
        k = B * i
        map_x.append(dot_x3(split2(wx_ref[k:, at(i)]), [e[k:] for e in cross], 0, 0))
        map_y.append(dot_x3([e[:, k:] for e in cross], split2(wy_ref[k:, at(i)])))
    high, low = split2(jnp.concatenate(map_x, 0))
    px_ref[...] = (dot(x_ref[...], high) + dot(x_ref[...], low)).astype(BF)
    high, low = split2(jnp.concatenate(map_y, 1))
    py_ref[...] = (dot(y_ref[...], high, 1, 1) + dot(y_ref[...], low, 1, 1)).astype(BF)


def params():
    return pltpu.CompilerParams(vmem_limit_bytes=VMEM_LIMIT)


def reduce_scatter(v, axis, n, step, index):
    rows = v.shape[0] // n
    block = lambda k: lax.dynamic_slice_in_dim(v, k * rows, rows, 0)
    total = block(index)
    for m in range(1, n):
        pairs = [(i, i ^ (m * step)) for i in range(n * step)]
        total = total + lax.ppermute(block(index ^ m), axis, pairs)
    return total


def all_gather(v, axis, n, step, index):
    parts = [v]
    for m in range(1, n):
        pairs = [(i, i ^ (m * step)) for i in range(n * step)]
        parts.append(lax.ppermute(v, axis, pairs))
    parts = jnp.stack(parts)
    return jnp.concatenate([lax.dynamic_index_in_dim(parts, index ^ k, 0, keepdims=False) for k in range(n)], 0)


def on_device(x_states, y_states):
    rows, width = x_states.shape
    n = width // B
    gr, gc = lax.axis_size("gr"), lax.axis_size("gc")
    chips = gr // 2
    total_rows = rows * gr * gc
    core = lax.axis_index("gr") % 2
    chip = lax.axis_index("gr") // 2
    plane = lax.axis_index("gc")
    swap = lambda v: lax.ppermute(v, "gr", [(i, i ^ 1) for i in range(gr)])
    core_arg = jnp.reshape(core, (1,)).astype(jnp.int32)
    smem = pl.BlockSpec(memory_space=pltpu.SMEM)
    vmem = pl.BlockSpec(memory_space=pltpu.VMEM)

    tri = B * len(upper_blocks(n))
    packed = tri + width * width // 2 // B

    def gram(partner):
        return pl.pallas_call(
            lambda *refs: gram_kernel(partner, *refs),
            out_shape=jax.ShapeDtypeStruct((packed, B), F32),
            in_specs=[smem, vmem, vmem],
            out_specs=vmem,
            scratch_shapes=[pltpu.VMEM((rows, width), BF)],
            compiler_params=params(),
            cost_estimate=pl.CostEstimate(flops=2 * rows * packed * B, bytes_accessed=4 * rows * width, transcendentals=0),
            name="gram_partner" if partner else "gram_own",
        )(core_arg, x_states, y_states)

    sums = swap(gram(True))
    sums = gram(False) + sums
    sums = reduce_scatter(sums, "gr", chips, 2, chip)
    sums = reduce_scatter(sums, "gc", gc, 1, plane)
    sums = all_gather(sums, "gc", gc, 1, plane)
    sums = all_gather(sums, "gr", chips, 2, chip)

    cov_xy = sums[tri:] / total_rows
    cov_xy_other = swap(cov_xy)
    white = pl.pallas_call(
        lambda *refs: factor_kernel(float(total_rows), n, *refs),
        out_shape=jax.ShapeDtypeStruct((tri, B), F32),
        in_specs=[vmem],
        out_specs=vmem,
        scratch_shapes=[pltpu.VMEM((width, width), F32)],
        compiler_params=params(),
        cost_estimate=pl.CostEstimate(flops=20_000_000_000, bytes_accessed=8 * tri * B, transcendentals=0),
        name="factor",
    )(sums[:tri])
    white_other = swap(white)

    return pl.pallas_call(
        project_kernel,
        out_shape=(
            jax.ShapeDtypeStruct((rows, width), BF),
            jax.ShapeDtypeStruct((rows, width), BF),
            jax.ShapeDtypeStruct((width, width), F32),
        ),
        in_specs=[smem] + [vmem] * 6,
        out_specs=(vmem,) * 3,
        scratch_shapes=[pltpu.VMEM((width, width), F32)] * 3,
        compiler_params=params(),
        cost_estimate=pl.CostEstimate(flops=8 * rows * width * width, bytes_accessed=16 * rows * width, transcendentals=0),
        name="project",
    )(core_arg, x_states, y_states, white, white_other, cov_xy, cov_xy_other)


def solution(mesh):
    return jax.shard_map(
        on_device,
        mesh=mesh,
        in_specs=(P(("gr", "gc"), None), P(("gr", "gc"), None)),
        out_specs=(P(("gr", "gc"), None), P(("gr", "gc"), None), P()),
        check_vma=False,
    )
```

```python
import jax
import jax.numpy as jnp
from jax import lax
from jax.experimental import pallas as pl
from jax.experimental.pallas import tpu as pltpu
from jax.sharding import PartitionSpec as P

RIDGE = 0.1
B = 128
NB = 16
BF = jnp.bfloat16
F32 = jnp.float32
COPIES = 8


def dot(a, b, ca=1, cb=0, precision=None):
    return lax.dot_general(a, b, (((ca,), (cb,)), ((), ())), preferred_element_type=F32, precision=precision)


def dot_f32(a, b, ca=1, cb=0):
    return dot(a, b, ca, cb, lax.Precision.HIGHEST)


def split2(a):
    high = a.astype(BF)
    return high, (a - high.astype(F32)).astype(BF)


def split3(a):
    high = a.astype(BF)
    rest = a - high.astype(F32)
    mid = rest.astype(BF)
    return high, mid, (rest - mid.astype(F32)).astype(BF)


def dot_x3(a, b, ca=1, cb=0):
    ah, al = a
    bh, bl = b
    return dot(ah, bh, ca, cb) + (dot(ah, bl, ca, cb) + dot(al, bh, ca, cb))


def outer_sum(u, v):
    uh, um, ul = split3(u)
    vh, vm, vl = split3(v)
    a = jnp.concatenate([uh, uh, um, uh, ul, um], 0)
    b = jnp.concatenate([vh, vm, vh, vl, vh, vm], 0)
    return dot(a, b, 0, 0)


def inverse_factor(a):
    n = a.shape[0]
    r = lax.broadcasted_iota(jnp.int32, (n, n), 0)
    c = lax.broadcasted_iota(jnp.int32, (n, n), 1)
    z = jnp.where(r == c, 1.0, 0.0).astype(F32)
    rows = lax.broadcasted_iota(jnp.int32, (NB, n), 0)
    out = []
    for s in range(n // NB):
        t, v = a[:NB], z[:NB]
        cols = [jnp.broadcast_to(t[:, NB * s + q : NB * s + q + 1], (NB, n)) for q in range(NB)]
        pivots = jnp.zeros((NB, n), F32)
        for k in range(NB):
            d = cols[k][k : k + 1, :]
            pivots = jnp.where(rows == k, d, pivots)
            if k == NB - 1:
                break
            m = jnp.where(rows > k, cols[k] * (1.0 / d), 0.0)
            t = t - m * t[k : k + 1, :]
            v = v - m * v[k : k + 1, :]
            for q in range(k + 1, NB):
                cols[q] = cols[q] - m * cols[q][k : k + 1, :]
        scale = lax.rsqrt(pivots)
        t, v = t * scale, v * scale
        out.append(v)
        if NB * (s + 1) < n:
            update = outer_sum(t[:, NB * (s + 1) :], jnp.concatenate([t, v], 1))
            a, z = a[NB:] - update[:, :n], z[NB:] - update[:, n:]
    return jnp.concatenate(out, 0)


def upper_blocks(n):
    return [(i, j) for i in range(n) for j in range(i, n)]


def lower_blocks(n):
    return [(i, j) for i in range(n) for j in range(i + 1)]


def write_upper(g_ref, o_ref):
    n = g_ref.shape[1] // B
    row = 0
    for i in range(n):
        g = dot(g_ref[:, B * i : B * (i + 1)], g_ref[:, B * i :], 0, 0)
        for j in range(n - i):
            o_ref[row : row + B, :] = g[:, B * j : B * (j + 1)]
            row += B


def gram_partner_kernel(core_ref, x_ref, y_ref, o_ref, a_ref, sems):
    chunk = a_ref.shape[0] // COPIES
    core = core_ref[0]
    copies = lambda ref: [
        pltpu.make_async_copy(ref.at[pl.ds(k * chunk, chunk)], a_ref.at[pl.ds(k * chunk, chunk)], sems.at[k])
        for k in range(COPIES)
    ]

    @pl.when(core == 0)
    def _():
        for copy in copies(y_ref):
            copy.start()

    @pl.when(core == 1)
    def _():
        for copy in copies(x_ref):
            copy.start()

    for copy in copies(x_ref):
        copy.wait()
    write_upper(a_ref, o_ref)


def gram_own_kernel(core_ref, x_ref, y_ref, o_ref, cm_ref, co_ref, a_ref):
    width = x_ref.shape[1]
    half = width // 2
    core = core_ref[0]

    @pl.when(core == 0)
    def _():
        a_ref[...] = x_ref[...]

    @pl.when(core == 1)
    def _():
        a_ref[...] = y_ref[...]

    write_upper(a_ref, o_ref)
    for owner, c_ref in ((1 - core, co_ref), (core, cm_ref)):
        g = dot(x_ref[...], y_ref[:, pl.ds(pl.multiple_of(owner * half, half), half)], 0, 0)
        for j in range(half // B):
            c_ref[width * j : width * (j + 1), :] = g[:, B * j : B * (j + 1)]


def factor_kernel(total_rows, n, s_ref, o_ref, f_ref):
    r = lax.broadcasted_iota(jnp.int32, (B, B), 0)
    c = lax.broadcasted_iota(jnp.int32, (B, B), 1)
    ridge = jnp.where(r == c, RIDGE, 0.0).astype(F32)
    at = lambda i: slice(B * i, B * (i + 1))
    for k, (i, j) in enumerate(upper_blocks(n)):
        block = s_ref[at(k), :] / total_rows
        f_ref[at(i), at(j)] = block + ridge if i == j else block
    for b in range(n):
        w = inverse_factor(f_ref[at(b), at(b)])
        f_ref[at(b), at(b)] = w
        if b > 0:
            f_ref[at(b), : B * b] = dot_f32(w, f_ref[at(b), : B * b])
        if b < n - 1:
            f_ref[at(b), B * (b + 1) :] = dot_f32(w, f_ref[at(b), B * (b + 1) :])
        for i in range(b + 1, n):
            u = f_ref[at(b), at(i)]
            f_ref[at(i), B * i :] -= dot_f32(u, f_ref[at(b), B * i :], 0, 0)
            if b > 0:
                f_ref[at(i), : B * b] -= dot_f32(u, f_ref[at(b), : B * b], 0, 0)
            f_ref[at(i), at(b)] = -dot_f32(u, w, 0, 0)
    for k, (i, j) in enumerate(lower_blocks(n)):
        o_ref[at(k), :] = f_ref[at(i), at(j)]


def project_kernel(core_ref, x_ref, y_ref, wm_ref, wo_ref, cm_ref, co_ref, px_ref, py_ref, cross_ref, wx_ref, wy_ref, c_ref):
    width = x_ref.shape[1]
    n = width // B
    half = width // 2
    core = core_ref[0]
    at = lambda i: slice(B * i, B * (i + 1))

    def unpack(w_x, w_y, c_0, c_1):
        for k, (i, j) in enumerate(lower_blocks(n)):
            wx_ref[at(i), at(j)] = w_x[at(k), :]
            wy_ref[at(i), at(j)] = w_y[at(k), :]
        for j in range(half // B):
            c_ref[:, B * j : B * (j + 1)] = c_0[width * j : width * (j + 1), :]
            c_ref[:, half + B * j : half + B * (j + 1)] = c_1[width * j : width * (j + 1), :]

    @pl.when(core == 0)
    def _():
        unpack(wm_ref, wo_ref, cm_ref, co_ref)

    @pl.when(core == 1)
    def _():
        unpack(wo_ref, wm_ref, co_ref, cm_ref)

    c_hl = split2(c_ref[...])
    left = []
    for i in range(n):
        k = B * (i + 1)
        left.append(dot_x3(split2(wx_ref[at(i), :k]), [e[:k] for e in c_hl]))
    left = split2(jnp.concatenate(left, 0))
    for j in range(n):
        k = B * (j + 1)
        cross_ref[:, at(j)] = dot_x3([e[:, :k] for e in left], split2(wy_ref[at(j), :k]), 1, 1)
    cross = split2(cross_ref[...])
    map_x, map_y = [], []
    for i in range(n):
        k = B * i
        map_x.append(dot_x3(split2(wx_ref[k:, at(i)]), [e[k:] for e in cross], 0, 0))
        map_y.append(dot_x3([e[:, k:] for e in cross], split2(wy_ref[k:, at(i)])))
    high, low = split2(jnp.concatenate(map_x, 0))
    px_ref[...] = (dot(x_ref[...], high) + dot(x_ref[...], low)).astype(BF)
    high, low = split2(jnp.concatenate(map_y, 1))
    py_ref[...] = (dot(y_ref[...], high, 1, 1) + dot(y_ref[...], low, 1, 1)).astype(BF)


def params(mib):
    return pltpu.CompilerParams(vmem_limit_bytes=mib * 1024 * 1024)


def shift(v, axis, m):
    return lax.ppermute(v, axis, [(i, i ^ m) for i in range(lax.axis_size(axis))])


def scatter_start(v, axis, n, step, index):
    rows = v.shape[0] // n
    block = lambda k: lax.dynamic_slice_in_dim(v, k * rows, rows, 0)
    return block(index), [shift(block(index ^ m), axis, m * step) for m in range(1, n)]


def scatter_end(state):
    total, parts = state
    for part in parts:
        total = total + part
    return total


def gather_start(v, axis, n, step):
    return [v] + [shift(v, axis, m * step) for m in range(1, n)]


def gather_end(parts, index):
    stacked = jnp.stack(parts)
    return jnp.concatenate([lax.dynamic_index_in_dim(stacked, index ^ k, 0, keepdims=False) for k in range(len(parts))], 0)


def on_device(x_states, y_states):
    rows, width = x_states.shape
    n = width // B
    gr, gc = lax.axis_size("gr"), lax.axis_size("gc")
    chips = gr // 2
    total_rows = rows * gr * gc
    core = lax.axis_index("gr") % 2
    chip = lax.axis_index("gr") // 2
    plane = lax.axis_index("gc")
    core_arg = jnp.reshape(core, (1,)).astype(jnp.int32)
    smem = pl.BlockSpec(memory_space=pltpu.SMEM)
    vmem = pl.BlockSpec(memory_space=pltpu.VMEM)
    hbm = pl.BlockSpec(memory_space=pltpu.HBM)
    tri = B * len(upper_blocks(n))
    half = width * width // 2 // B

    cov = pl.pallas_call(
        gram_partner_kernel,
        out_shape=jax.ShapeDtypeStruct((tri, B), F32),
        in_specs=[smem, hbm, hbm],
        out_specs=vmem,
        scratch_shapes=[pltpu.VMEM((rows, width), BF), pltpu.SemaphoreType.DMA((COPIES,))],
        compiler_params=params(6),
        cost_estimate=pl.CostEstimate(flops=2 * rows * tri * B, bytes_accessed=2 * rows * width, transcendentals=0),
        name="gram_partner",
    )(core_arg, x_states, y_states)
    x_again, y_again, cov = lax.optimization_barrier((x_states, y_states, cov))
    cov_in = shift(cov, "gr", 1)
    cov, cxy_own, cxy_other = pl.pallas_call(
        gram_own_kernel,
        out_shape=(
            jax.ShapeDtypeStruct((tri, B), F32),
            jax.ShapeDtypeStruct((half, B), F32),
            jax.ShapeDtypeStruct((half, B), F32),
        ),
        in_specs=[smem, vmem, vmem],
        out_specs=(vmem,) * 3,
        scratch_shapes=[pltpu.VMEM((rows, width), BF)],
        compiler_params=params(10),
        cost_estimate=pl.CostEstimate(flops=2 * rows * (tri + 2 * half) * B, bytes_accessed=8 * rows * width, transcendentals=0),
        name="gram_own",
    )(core_arg, x_again, y_again)

    cxy_in = shift(cxy_other, "gr", 1)
    cov, cxy_own = cov + cov_in, cxy_own + cxy_in
    blocks = lambda v: jnp.reshape(v, (chips * gc, -1, B))
    sums = jnp.reshape(jnp.concatenate([blocks(cov), blocks(cxy_own)], 1), (-1, B))
    sums = scatter_end(scatter_start(sums, "gr", chips, 2, chip))
    sums = scatter_end(scatter_start(sums, "gc", gc, 1, plane))
    sums = gather_end(gather_start(sums, "gc", gc, 1), plane)
    sums = jnp.reshape(sums, (gc, -1, B))
    own = tri // (chips * gc)
    cov = gather_start(jnp.reshape(sums[:, :own], (-1, B)), "gr", chips, 2)
    cxy = gather_start(jnp.reshape(sums[:, own:], (-1, B)), "gr", chips, 2)
    cov = gather_end(cov, chip)

    white = pl.pallas_call(
        lambda *refs: factor_kernel(float(total_rows), n, *refs),
        out_shape=jax.ShapeDtypeStruct((tri, B), F32),
        in_specs=[vmem],
        out_specs=vmem,
        scratch_shapes=[pltpu.VMEM((width, width), F32)],
        compiler_params=params(8),
        cost_estimate=pl.CostEstimate(flops=20_000_000_000, bytes_accessed=8 * tri * B, transcendentals=0),
        name="factor",
    )(cov)
    cxy, white = lax.optimization_barrier((cxy, white))
    cxy = gather_end(cxy, chip) / total_rows
    cxy_other = shift(cxy, "gr", 1)
    white_other = shift(white, "gr", 1)

    return pl.pallas_call(
        project_kernel,
        out_shape=(
            jax.ShapeDtypeStruct((rows, width), BF),
            jax.ShapeDtypeStruct((rows, width), BF),
            jax.ShapeDtypeStruct((width, width), F32),
        ),
        in_specs=[smem] + [vmem] * 6,
        out_specs=(vmem,) * 3,
        scratch_shapes=[pltpu.VMEM((width, width), F32)] * 3,
        compiler_params=params(32),
        cost_estimate=pl.CostEstimate(flops=8 * rows * width * width, bytes_accessed=16 * rows * width, transcendentals=0),
        name="project",
    )(core_arg, x_states, y_states, white, white_other, cxy, cxy_other)


def solution(mesh):
    return jax.shard_map(
        on_device,
        mesh=mesh,
        in_specs=(P(("gr", "gc"), None), P(("gr", "gc"), None)),
        out_specs=(P(("gr", "gc"), None), P(("gr", "gc"), None), P()),
        check_vma=False,
    )
```

```python
import jax
import jax.numpy as jnp
from jax import lax
from jax.experimental import pallas as pl
from jax.experimental.pallas import tpu as pltpu
from jax.sharding import PartitionSpec as P

RIDGE = 0.1
B = 128
NB = 16
TILE = 8
BF = jnp.bfloat16
F32 = jnp.float32
CHUNKS = 2


def dot(a, b, ca=1, cb=0, precision=None):
    return lax.dot_general(a, b, (((ca,), (cb,)), ((), ())), preferred_element_type=F32, precision=precision)


def dot_f32(a, b, ca=1, cb=0):
    return dot(a, b, ca, cb, lax.Precision.HIGHEST)


def split2(a):
    high = a.astype(BF)
    return high, (a - high.astype(F32)).astype(BF)


def split3(a):
    high = a.astype(BF)
    rest = a - high.astype(F32)
    mid = rest.astype(BF)
    return high, mid, (rest - mid.astype(F32)).astype(BF)


def dot_x3(a, b, ca=1, cb=0):
    ah, al = a
    bh, bl = b
    return dot(jnp.concatenate([ah, ah, al], ca), jnp.concatenate([bh, bl, bh], cb), ca, cb)


def outer_sum(u, v):
    uh, um, ul = split3(u)
    vh, vm, vl = split3(v)
    a = jnp.concatenate([uh, uh, um, uh, ul, um], 0)
    b = jnp.concatenate([vh, vm, vh, vl, vh, vm], 0)
    return dot(a, b, 0, 0)


def inverse_factor(a, beside=()):
    beside = list(beside)
    n = a.shape[0]
    panels = n // NB
    r = lax.broadcasted_iota(jnp.int32, (n, n), 0)
    c = lax.broadcasted_iota(jnp.int32, (n, n), 1)
    z = jnp.where(r == c, 1.0, 0.0).astype(F32)
    sublane = lax.broadcasted_iota(jnp.int32, (TILE, n), 0)
    tiles = lambda a, z: [(a[k : k + TILE], z[k : k + TILE]) for k in range(0, NB, TILE)]
    now, later, rest = tiles(a[:NB], z[:NB]), tiles(a[NB : 2 * NB], z[NB : 2 * NB]), (a[2 * NB :], z[2 * NB :])
    out = []
    for s in range(panels):
        last = s == panels - 1
        groups = now if last else now + later
        left = [g[0] for g in groups]
        right = [g[1] for g in groups]
        cols = [[jnp.broadcast_to(g[:, NB * s + q : NB * s + q + 1], (TILE, n)) for q in range(NB)] for g in left]
        pivots = [jnp.ones((TILE, n), F32) for _ in now]
        for k in range(NB):
            tile, sub = divmod(k, TILE)
            row = lambda v: v[sub : sub + 1, :]
            d = row(cols[tile][k])
            pivots[tile] = jnp.where(sublane == sub, d, pivots[tile])
            inverse = 1.0 / d
            left_row, right_row = row(left[tile]), row(right[tile])
            entries = {q: row(cols[tile][q]) for q in range(k + 1, NB)}
            for g in range(tile, len(groups)):
                if g == tile and sub == TILE - 1:
                    continue
                m = cols[g][k] * inverse
                if g == tile:
                    m = jnp.where(sublane > sub, m, 0.0)
                for q in range(k + 1, NB):
                    cols[g][q] = cols[g][q] - m * entries[q]
                left[g] = left[g] - m * left_row
                right[g] = right[g] - m * right_row
        scales = [lax.rsqrt(p) for p in pivots]
        u = jnp.concatenate([v * scale for v, scale in zip(left, scales)], 0)
        v = jnp.concatenate([v * scale for v, scale in zip(right, scales)], 0)
        out.append(v)
        now = list(zip(left, right))[len(now) :]
        if s < panels - 2:
            update = outer_sum(u[:, NB * (s + 2) :], jnp.concatenate([u, v], 1))
            a, z = rest[0] - update[:, :n], rest[1] - update[:, n:]
            later, rest = tiles(a[:NB], z[:NB]), (a[NB:], z[NB:])
        if beside:
            beside.pop(0)()
    for work in beside:
        work()
    return jnp.concatenate(out, 0)


def upper_blocks(n):
    return [(i, j) for i in range(n) for j in range(i, n)]


def lower_blocks(n):
    return [(i, j) for i in range(n) for j in range(i + 1)]


def gram_kernel(core_ref, x_ref, y_ref, other_ref, own_ref, a_ref):
    width = x_ref.shape[1]
    half = width // 2
    n = width // B
    core = core_ref[0]
    for owner, o_ref in ((1 - core, other_ref), (core, own_ref)):

        @pl.when(owner == 0)
        def _():
            a_ref[...] = x_ref[...]

        @pl.when(owner == 1)
        def _():
            a_ref[...] = y_ref[...]

        row = 0
        for i in range(n):
            g = dot(a_ref[:, B * i : B * (i + 1)], a_ref[:, B * i :], 0, 0)
            for j in range(n - i):
                o_ref[row : row + B, :] = g[:, B * j : B * (j + 1)]
                row += B
        g = dot(x_ref[...], y_ref[:, pl.ds(pl.multiple_of(owner * half, half), half)], 0, 0)
        for j in range(half // B):
            o_ref[row : row + width, :] = g[:, B * j : B * (j + 1)]
            row += width


def factor_kernel(total_rows, n, s_ref, o_ref, f_ref):
    r = lax.broadcasted_iota(jnp.int32, (B, B), 0)
    c = lax.broadcasted_iota(jnp.int32, (B, B), 1)
    ridge = jnp.where(r == c, RIDGE, 0.0).astype(F32)
    at = lambda i: slice(B * i, B * (i + 1))
    for k, (i, j) in enumerate(upper_blocks(n)):
        block = s_ref[at(k), :] / total_rows
        f_ref[at(i), at(j)] = block + ridge if i == j else block
    beside = []
    a = f_ref[at(0), at(0)]
    for b in range(n):
        w = inverse_factor(a, beside)
        f_ref[at(b), at(b)] = w
        if b == n - 1:
            f_ref[at(b), : B * b] = dot_f32(w, f_ref[at(b), : B * b])
            break
        u = dot_f32(w, f_ref[at(b), at(b + 1)])
        f_ref[at(b), at(b + 1)] = u
        a = f_ref[at(b + 1), at(b + 1)] - dot_f32(u, u, 0, 0)

        def rows(b=b, w=w):
            if b > 0:
                f_ref[at(b), : B * b] = dot_f32(w, f_ref[at(b), : B * b])
            if b + 2 < n:
                f_ref[at(b), B * (b + 2) :] = dot_f32(w, f_ref[at(b), B * (b + 2) :])

        def below(i, b=b, w=w):
            u = f_ref[at(b), at(i)]
            first = B * i if i > b + 1 else B * (i + 1)
            if first < B * n:
                f_ref[at(i), first:] -= dot_f32(u, f_ref[at(b), first:], 0, 0)
            if b > 0:
                f_ref[at(i), : B * b] -= dot_f32(u, f_ref[at(b), : B * b], 0, 0)
            f_ref[at(i), at(b)] = -dot_f32(u, w, 0, 0)

        beside = [rows] + [lambda i=i, below=below: below(i) for i in range(b + 1, n)]
    for k, (i, j) in enumerate(lower_blocks(n)):
        o_ref[at(k), :] = f_ref[at(i), at(j)]


def project_kernel(
    core_ref, x_ref, y_ref, wm_ref, wo_ref, cm_ref, co_ref, px_hbm, py_hbm, cross_hbm,
    px_ref, py_ref, cross_ref, wx_ref, wy_ref, c_ref, sems,
):
    rows, width = x_ref.shape
    n = width // B
    half = width // 2
    core = core_ref[0]
    at = lambda i: slice(B * i, B * (i + 1))

    def unpack(w_x, w_y, c_0, c_1):
        for k, (i, j) in enumerate(lower_blocks(n)):
            wx_ref[at(i), at(j)] = w_x[at(k), :]
            wy_ref[at(i), at(j)] = w_y[at(k), :]
        for j in range(half // B):
            c_ref[:, B * j : B * (j + 1)] = c_0[width * j : width * (j + 1), :]
            c_ref[:, half + B * j : half + B * (j + 1)] = c_1[width * j : width * (j + 1), :]

    @pl.when(core == 0)
    def _():
        unpack(wm_ref, wo_ref, cm_ref, co_ref)

    @pl.when(core == 1)
    def _():
        unpack(wo_ref, wm_ref, co_ref, cm_ref)

    c_hl = split2(c_ref[...])
    left = []
    for i in range(n):
        k = B * (i + 1)
        left.append(dot_x3(split2(wx_ref[at(i), :k]), [e[:k] for e in c_hl]))
    left = split2(jnp.concatenate(left, 0))
    for j in range(n):
        k = B * (j + 1)
        cross_ref[:, at(j)] = dot_x3([e[:, :k] for e in left], split2(wy_ref[at(j), :k]), 1, 1)
    copies = [pltpu.make_async_copy(cross_ref, cross_hbm, sems.at[0])]
    copies[0].start()
    cross = split2(cross_ref[...])
    map_x, map_y = [], []
    for i in range(n):
        k = B * i
        map_x.append(dot_x3(split2(wx_ref[k:, at(i)]), [e[k:] for e in cross], 0, 0))
        map_y.append(dot_x3([e[:, k:] for e in cross], split2(wy_ref[k:, at(i)])))
    map_x, map_y = jnp.concatenate(map_x, 0), jnp.concatenate(map_y, 1)
    step = rows // CHUNKS
    for ref, p_ref, p_hbm, m, cb in ((x_ref, px_ref, px_hbm, map_x, 0), (y_ref, py_ref, py_hbm, map_y, 1)):
        m = jnp.concatenate(split2(m), cb)
        for k in range(CHUNKS):
            part = pl.ds(k * step, step)
            v = ref[part, :]
            p_ref[part, :] = dot(jnp.concatenate([v, v], 1), m, 1, cb).astype(BF)
            copies.append(pltpu.make_async_copy(p_ref.at[part], p_hbm.at[part], sems.at[len(copies)]))
            copies[-1].start()
    for copy in copies:
        copy.wait()


def params(mib):
    return pltpu.CompilerParams(vmem_limit_bytes=mib * 1024 * 1024)


def shift(v, axis, m):
    return lax.ppermute(v, axis, [(i, i ^ m) for i in range(lax.axis_size(axis))])


def scatter_start(v, axis, n, step, index):
    rows = v.shape[0] // n
    block = lambda k: lax.dynamic_slice_in_dim(v, k * rows, rows, 0)
    return block(index), [shift(block(index ^ m), axis, m * step) for m in range(1, n)]


def scatter_end(state):
    total, parts = state
    for part in parts:
        total = total + part
    return total


def gather_start(v, axis, n, step):
    return [v] + [shift(v, axis, m * step) for m in range(1, n)]


def gather_end(parts, place):
    stacked = jnp.stack(parts)
    return jnp.concatenate([lax.dynamic_index_in_dim(stacked, p, 0, keepdims=False) for p in place], 0)


def plane_scatter(v, chips, core, chip):
    bits = chips.bit_length() - 1
    for s in range(bits):
        masks = 1 << s, 1 << (bits - 1 - s)
        mask = jnp.where(core == 0, *masks)
        bit = (chip & mask) // mask
        rows = v.shape[0] // 2
        half = lambda k: lax.dynamic_slice_in_dim(v, k * rows, rows, 0)
        pairs = [(i, i ^ (2 * masks[i % 2])) for i in range(2 * chips)]
        v = half(bit) + lax.ppermute(half(1 - bit), "gr", pairs)
    reverse = lambda k: sum(((k >> b) & 1) << (bits - 1 - b) for b in range(bits))
    return v, [chip ^ jnp.where(core == 0, reverse(k), k) for k in range(chips)]


def on_device(x_states, y_states):
    rows, width = x_states.shape
    n = width // B
    gr, gc = lax.axis_size("gr"), lax.axis_size("gc")
    chips = gr // 2
    total_rows = rows * gr * gc
    core = lax.axis_index("gr") % 2
    chip = lax.axis_index("gr") // 2
    plane = lax.axis_index("gc")
    core_arg = jnp.reshape(core, (1,)).astype(jnp.int32)
    smem = pl.BlockSpec(memory_space=pltpu.SMEM)
    vmem = pl.BlockSpec(memory_space=pltpu.VMEM)
    hbm = pl.BlockSpec(memory_space=pltpu.HBM)
    tri = B * len(upper_blocks(n))
    half = width * width // 2 // B

    panel = pltpu.VMEM((rows, width), BF)

    other, own = pl.pallas_call(
        gram_kernel,
        out_shape=(jax.ShapeDtypeStruct((tri + half, B), F32),) * 2,
        in_specs=[smem, vmem, vmem],
        out_specs=(vmem,) * 2,
        scratch_shapes=[panel],
        compiler_params=params(10),
        cost_estimate=pl.CostEstimate(flops=4 * rows * (tri + half) * B, bytes_accessed=8 * rows * width, transcendentals=0),
        name="gram",
    )(core_arg, x_states, y_states)
    sums = own + shift(other, "gr", 1)
    cov, cxy = sums[:tri], sums[tri:]
    blocks = lambda v: jnp.reshape(v, (chips * gc, -1, B))
    sums = jnp.reshape(jnp.concatenate([blocks(cov), blocks(cxy)], 1), (-1, B))
    sums, place = plane_scatter(sums, chips, core, chip)
    sums = scatter_end(scatter_start(sums, "gc", gc, 1, plane))
    sums = gather_end(gather_start(sums, "gc", gc, 1), [plane ^ k for k in range(gc)])
    sums = jnp.reshape(sums, (gc, -1, B))
    own = tri // (chips * gc)
    cov = gather_start(jnp.reshape(sums[:, :own], (-1, B)), "gr", chips, 2)
    cxy = gather_start(jnp.reshape(sums[:, own:], (-1, B)), "gr", chips, 2)
    cov = gather_end(cov, place)

    white = pl.pallas_call(
        lambda *refs: factor_kernel(float(total_rows), n, *refs),
        out_shape=jax.ShapeDtypeStruct((tri, B), F32),
        in_specs=[vmem],
        out_specs=vmem,
        scratch_shapes=[pltpu.VMEM((width, width), F32)],
        compiler_params=params(8),
        cost_estimate=pl.CostEstimate(flops=20_000_000_000, bytes_accessed=8 * tri * B, transcendentals=0),
        name="factor",
    )(cov)
    cxy, white = lax.optimization_barrier((cxy, white))
    cxy = gather_end(cxy, place) / total_rows
    cxy_other = shift(cxy, "gr", 1)
    white_other = shift(white, "gr", 1)

    return pl.pallas_call(
        project_kernel,
        out_shape=(
            jax.ShapeDtypeStruct((rows, width), BF),
            jax.ShapeDtypeStruct((rows, width), BF),
            jax.ShapeDtypeStruct((width, width), F32),
        ),
        in_specs=[smem] + [vmem] * 6,
        out_specs=(hbm,) * 3,
        scratch_shapes=[panel] * 2 + [pltpu.VMEM((width, width), F32)] * 4 + [pltpu.SemaphoreType.DMA((1 + 2 * CHUNKS,))],
        compiler_params=params(24),
        cost_estimate=pl.CostEstimate(flops=8 * rows * width * width, bytes_accessed=16 * rows * width, transcendentals=0),
        name="project",
    )(core_arg, x_states, y_states, white, white_other, cxy, cxy_other)


def solution(mesh):
    return jax.shard_map(
        on_device,
        mesh=mesh,
        in_specs=(P(("gr", "gc"), None), P(("gr", "gc"), None)),
        out_specs=(P(("gr", "gc"), None), P(("gr", "gc"), None), P()),
        check_vma=False,
    )
```

```python
import jax
import jax.numpy as jnp
from jax import lax
from jax.experimental import pallas as pl
from jax.experimental.pallas import tpu as pltpu
from jax.sharding import PartitionSpec as P

RIDGE = 0.1
B = 128
NB = 16
TILE = 8
BF = jnp.bfloat16
F32 = jnp.float32
CHUNKS = 2


def dot(a, b, ca=1, cb=0, precision=None):
    return lax.dot_general(a, b, (((ca,), (cb,)), ((), ())), preferred_element_type=F32, precision=precision)


def dot_f32(a, b, ca=1, cb=0):
    return dot(a, b, ca, cb, lax.Precision.HIGHEST)


def split2(a):
    high = a.astype(BF)
    return high, (a - high.astype(F32)).astype(BF)


def split3(a):
    high = a.astype(BF)
    rest = a - high.astype(F32)
    mid = rest.astype(BF)
    return high, mid, (rest - mid.astype(F32)).astype(BF)


def dot_x3(a, b, ca=1, cb=0):
    ah, al = a
    bh, bl = b
    return dot(jnp.concatenate([ah, ah, al], ca), jnp.concatenate([bh, bl, bh], cb), ca, cb)


def outer_sum(u, v):
    uh, um, ul = split3(u)
    vh, vm, vl = split3(v)
    a = jnp.concatenate([uh, uh, um, uh, ul, um], 0)
    b = jnp.concatenate([vh, vm, vh, vl, vh, vm], 0)
    return dot(a, b, 0, 0)


def inverse_factor(a, beside=()):
    beside = list(beside)
    n = a.shape[0]
    panels = n // NB
    sublane = lax.broadcasted_iota(jnp.int32, (TILE, n), 0)
    lane = lax.broadcasted_iota(jnp.int32, (TILE, n), 1)
    tiles = lambda a: [a[k : k + TILE] for k in range(0, NB, TILE)]
    row = lambda v, k: v[k : k + 1, :]
    now, later, rest = tiles(a[:NB]), tiles(a[NB : 2 * NB]), a[2 * NB :]
    out = []
    for s in range(panels):
        base = NB * s
        groups = now if s == panels - 1 else now + later
        cols = [
            {q: jnp.broadcast_to(v[:, base + q : base + q + 1], (TILE, n)) for q in range(min(NB, TILE * (g + 1)))}
            for g, v in enumerate(groups)
        ]
        inside = (lane >= base) & (lane < base + NB)
        start = lambda g: jnp.where(lane - base - TILE * g == sublane, 1.0, 0.0) if g < len(now) else 0.0
        values = [jnp.where(inside, start(g), v) for g, v in enumerate(groups)]
        pivots = [jnp.ones((TILE, n), F32) for _ in now]
        for k in range(NB):
            tile, sub = divmod(k, TILE)
            d = row(cols[tile][k], sub)
            pivots[tile] = jnp.where(sublane == sub, d, pivots[tile])
            inverse = 1.0 / d
            pivot_row = row(values[tile], sub)
            entries = {q: row(cols[q // TILE][k], q % TILE) for q in range(k + 1, NB)}
            for g in range(tile, len(groups)):
                if g == tile and sub == TILE - 1:
                    continue
                m = cols[g][k] * inverse
                for q in range(k + 1, NB):
                    if q in cols[g]:
                        cols[g][q] = cols[g][q] - m * entries[q]
                if g == tile:
                    m = jnp.where(sublane > sub, m, 0.0)
                values[g] = values[g] - m * pivot_row
        u = jnp.concatenate([v * lax.rsqrt(p) for v, p in zip(values, pivots)], 0)
        out.append(u)
        now = values[len(now) :]
        if s < panels - 2:
            rest = jnp.where(inside[:1], 0.0, rest) - outer_sum(u[:, base + 2 * NB :], u)
            later, rest = tiles(rest[:NB]), rest[NB:]
        if beside:
            beside.pop(0)()
    for work in beside:
        work()
    r = lax.broadcasted_iota(jnp.int32, (n, n), 0)
    c = lax.broadcasted_iota(jnp.int32, (n, n), 1)
    return jnp.where(r >= c, jnp.concatenate(out, 0), 0.0)


def off_diagonal(n):
    return [(i, j) for i in range(n) for j in range(i + 1, n)]


def lower_blocks(n):
    return [(i, j) for i in range(n) for j in range(i + 1)]


def block_iotas():
    return lax.broadcasted_iota(jnp.int32, (B, B), 0), lax.broadcasted_iota(jnp.int32, (B, B), 1)


def folded_rows(n):
    return B * (n // 2 + n * (n - 1) // 2)


def fold(v_ref, o_ref, e_ref):
    n = v_ref.shape[1] // B
    r, c = block_iotas()
    diagonals = []
    for i in range(n):
        g = dot(v_ref[:, B * i : B * (i + 1)], v_ref[:, B * i :], 0, 0)
        diagonals.append(g[:, :B])
        for j in range(i + 1, n):
            k = n // 2 + off_diagonal(n).index((i, j))
            o_ref[B * k : B * (k + 1), :] = g[:, B * (j - i) : B * (j - i + 1)]
    extra = jnp.zeros((TILE, B), F32)
    for p in range(n // 2):
        low, high = diagonals[2 * p], diagonals[2 * p + 1]
        o_ref[B * p : B * (p + 1), :] = jnp.where(r >= c, low, high)
        diagonal = jnp.sum(jnp.where(r == c, high, 0.0), 0, keepdims=True)
        extra = jnp.where(lax.broadcasted_iota(jnp.int32, (TILE, B), 0) == p, diagonal, extra)
    e_ref[...] = jnp.zeros_like(e_ref)
    e_ref[:TILE, :] = extra


def gram_kernel(core_ref, x_ref, y_ref, other_ref, own_ref, gx_ref, ex_ref, gy_ref, ey_ref):
    width = x_ref.shape[1]
    half = width // 2
    core = core_ref[0]
    rows = gx_ref.shape[0]
    fold(x_ref, gx_ref, ex_ref)
    fold(y_ref, gy_ref, ey_ref)

    def write(o_ref, g_ref, e_ref):
        o_ref[:rows, :] = g_ref[...]
        o_ref[o_ref.shape[0] - B :, :] = e_ref[...]

    @pl.when(core == 0)
    def _():
        write(own_ref, gx_ref, ex_ref)
        write(other_ref, gy_ref, ey_ref)

    @pl.when(core == 1)
    def _():
        write(own_ref, gy_ref, ey_ref)
        write(other_ref, gx_ref, ex_ref)

    for owner, o_ref in ((1 - core, other_ref), (core, own_ref)):
        g = dot(x_ref[...], y_ref[:, pl.ds(pl.multiple_of(owner * half, half), half)], 0, 0)
        for j in range(half // B):
            o_ref[rows + width * j : rows + width * (j + 1), :] = g[:, B * j : B * (j + 1)]


def factor_kernel(total_rows, n, s_ref, e_ref, o_ref, f_ref):
    r, c = block_iotas()
    at = lambda i: slice(B * i, B * (i + 1))
    finish = lambda sums: sums / total_rows + jnp.where(r == c, RIDGE, 0.0)
    for p in range(n // 2):
        pair = s_ref[at(p), :]
        turned = pair.T
        f_ref[at(2 * p), at(2 * p)] = finish(jnp.where(r >= c, pair, turned))
        high = jnp.where(r == c, e_ref[p : p + 1, :], jnp.where(r < c, pair, turned))
        f_ref[at(2 * p + 1), at(2 * p + 1)] = finish(high)
    for k, (i, j) in enumerate(off_diagonal(n)):
        f_ref[at(i), at(j)] = s_ref[at(n // 2 + k), :] / total_rows
    beside = []
    a = f_ref[at(0), at(0)]
    for b in range(n):
        w = inverse_factor(a, beside)
        f_ref[at(b), at(b)] = w
        if b == n - 1:
            f_ref[at(b), : B * b] = dot_f32(w, f_ref[at(b), : B * b])
            break
        u = dot_f32(w, f_ref[at(b), at(b + 1)])
        f_ref[at(b), at(b + 1)] = u
        a = f_ref[at(b + 1), at(b + 1)] - dot_f32(u, u, 0, 0)

        def rows(b=b, w=w):
            if b > 0:
                f_ref[at(b), : B * b] = dot_f32(w, f_ref[at(b), : B * b])
            if b + 2 < n:
                f_ref[at(b), B * (b + 2) :] = dot_f32(w, f_ref[at(b), B * (b + 2) :])

        def below(i, b=b, w=w):
            u = f_ref[at(b), at(i)]
            first = B * i if i > b + 1 else B * (i + 1)
            if first < B * n:
                f_ref[at(i), first:] -= dot_f32(u, f_ref[at(b), first:], 0, 0)
            if b > 0:
                f_ref[at(i), : B * b] -= dot_f32(u, f_ref[at(b), : B * b], 0, 0)
            f_ref[at(i), at(b)] = -dot_f32(u, w, 0, 0)

        beside = [rows] + [lambda i=i, below=below: below(i) for i in range(b + 1, n)]
    for k, (i, j) in enumerate(lower_blocks(n)):
        o_ref[at(k), :] = f_ref[at(i), at(j)]


def project_kernel(
    core_ref, x_ref, y_ref, wm_ref, wo_ref, cm_ref, co_ref, px_hbm, py_hbm, cross_hbm,
    px_ref, py_ref, cross_ref, wx_ref, wy_ref, c_ref, sems,
):
    rows, width = x_ref.shape
    n = width // B
    half = width // 2
    core = core_ref[0]
    at = lambda i: slice(B * i, B * (i + 1))

    def unpack(w_x, w_y, c_0, c_1):
        for w_ref, w in ((wx_ref, w_x), (wy_ref, w_y)):
            for i in range(0, n, 2):
                w_ref[at(i), at(i + 1)] = jnp.zeros((B, B), F32)
            for k, (i, j) in enumerate(lower_blocks(n)):
                w_ref[at(i), at(j)] = w[at(k), :]
        for j in range(half // B):
            c_ref[:, at(j)] = c_0[width * j : width * (j + 1), :]
            c_ref[:, half + B * j : half + B * (j + 1)] = c_1[width * j : width * (j + 1), :]

    @pl.when(core == 0)
    def _():
        unpack(wm_ref, wo_ref, cm_ref, co_ref)

    @pl.when(core == 1)
    def _():
        unpack(wo_ref, wm_ref, co_ref, cm_ref)

    ends = range(0, width, 2 * B)
    c_hl = split2(c_ref[...])
    left = []
    for i in ends:
        k = i + 2 * B
        left.append(dot_x3(split2(wx_ref[i:k, :k]), [e[:k] for e in c_hl]))
    left = split2(jnp.concatenate(left, 0))
    for i in ends:
        k = i + 2 * B
        cross_ref[:, i:k] = dot_x3([e[:, :k] for e in left], split2(wy_ref[i:k, :k]), 1, 1)
    copies = [pltpu.make_async_copy(cross_ref, cross_hbm, sems.at[0])]
    copies[0].start()
    cross = split2(cross_ref[...])
    map_x, map_y = [], []
    for i in ends:
        columns = slice(i, i + 2 * B)
        map_x.append(dot_x3(split2(wx_ref[i:, columns]), [e[i:] for e in cross], 0, 0))
        map_y.append(dot_x3([e[:, i:] for e in cross], split2(wy_ref[i:, columns])))
    map_x, map_y = jnp.concatenate(map_x, 0), jnp.concatenate(map_y, 1)
    step = rows // CHUNKS
    for ref, p_ref, p_hbm, m, cb in ((x_ref, px_ref, px_hbm, map_x, 0), (y_ref, py_ref, py_hbm, map_y, 1)):
        m = jnp.concatenate(split2(m), cb)
        for k in range(CHUNKS):
            part = pl.ds(k * step, step)
            v = ref[part, :]
            p_ref[part, :] = dot(jnp.concatenate([v, v], 1), m, 1, cb).astype(BF)
            copies.append(pltpu.make_async_copy(p_ref.at[part], p_hbm.at[part], sems.at[len(copies)]))
            copies[-1].start()
    for copy in copies:
        copy.wait()


def params(mib):
    return pltpu.CompilerParams(vmem_limit_bytes=mib * 1024 * 1024)


def shift(v, axis, m):
    return lax.ppermute(v, axis, [(i, i ^ m) for i in range(lax.axis_size(axis))])


def scatter_start(v, axis, n, step, index):
    rows = v.shape[0] // n
    block = lambda k: lax.dynamic_slice_in_dim(v, k * rows, rows, 0)
    return block(index), [shift(block(index ^ m), axis, m * step) for m in range(1, n)]


def scatter_end(state):
    total, parts = state
    for part in parts:
        total = total + part
    return total


def gather_start(v, axis, n, step):
    return [v] + [shift(v, axis, m * step) for m in range(1, n)]


def gather_end(parts, place):
    stacked = jnp.stack(parts)
    return jnp.concatenate([lax.dynamic_index_in_dim(stacked, p, 0, keepdims=False) for p in place], 0)


def plane_scatter(v, chips, core, chip):
    bits = chips.bit_length() - 1
    for s in range(bits):
        masks = 1 << s, 1 << (bits - 1 - s)
        mask = jnp.where(core == 0, *masks)
        bit = (chip & mask) // mask
        rows = v.shape[0] // 2
        half = lambda k: lax.dynamic_slice_in_dim(v, k * rows, rows, 0)
        pairs = [(i, i ^ (2 * masks[i % 2])) for i in range(2 * chips)]
        v = half(bit) + lax.ppermute(half(1 - bit), "gr", pairs)
    reverse = lambda k: sum(((k >> b) & 1) << (bits - 1 - b) for b in range(bits))
    return v, [(k, reverse(k)) for k in range(chips)]


def on_device(x_states, y_states):
    rows, width = x_states.shape
    n = width // B
    gr, gc = lax.axis_size("gr"), lax.axis_size("gc")
    chips = gr // 2
    total_rows = rows * gr * gc
    core = lax.axis_index("gr") % 2
    chip = lax.axis_index("gr") // 2
    plane = lax.axis_index("gc")
    core_arg = jnp.reshape(core, (1,)).astype(jnp.int32)
    smem = pl.BlockSpec(memory_space=pltpu.SMEM)
    vmem = pl.BlockSpec(memory_space=pltpu.VMEM)
    hbm = pl.BlockSpec(memory_space=pltpu.HBM)
    folded = folded_rows(n)
    half = width * width // 2 // B
    panel = pltpu.VMEM((rows, width), BF)
    gram = pltpu.VMEM((folded, B), F32)
    extra = pltpu.VMEM((B, B), F32)
    packed = jax.ShapeDtypeStruct((folded + half + B, B), F32)

    other, own = pl.pallas_call(
        gram_kernel,
        out_shape=(packed,) * 2,
        in_specs=[smem, vmem, vmem],
        out_specs=(vmem,) * 2,
        scratch_shapes=[gram, extra] * 2,
        compiler_params=params(10),
        cost_estimate=pl.CostEstimate(flops=4 * rows * (folded + half) * B, bytes_accessed=8 * rows * width, transcendentals=0),
        name="gram",
    )(core_arg, x_states, y_states)
    sums = own + shift(other, "gr", 1)
    shards = chips * gc
    blocks = lambda v: jnp.reshape(v, (shards, -1, B))
    flat = lambda v: jnp.reshape(v, (-1, B))
    parts = sums[:folded], sums[folded + half :], sums[folded : folded + half]
    sums = flat(jnp.concatenate([blocks(v) for v in parts], 1))
    sums, place = plane_scatter(sums, chips, core, chip)
    place_other = [chip ^ jnp.where(core == 0, a, b) for a, b in place]
    place = [chip ^ jnp.where(core == 0, b, a) for a, b in place]
    sums = scatter_end(scatter_start(sums, "gc", gc, 1, plane))
    sums = gather_end(gather_start(sums, "gc", gc, 1), [plane ^ k for k in range(gc)])
    sums = jnp.reshape(sums, (gc, -1, B))
    sizes = folded // shards, (folded + B) // shards
    cov = gather_start(flat(sums[:, : sizes[1]]), "gr", chips, 2)
    cxy = flat(sums[:, sizes[1] :])
    cxy = gather_start(jnp.stack([cxy, shift(cxy, "gr", 1)]), "gr", chips, 2)
    cov = jnp.reshape(gather_end(cov, place), (shards, -1, B))
    cov, extra = flat(cov[:, : sizes[0]]), flat(cov[:, sizes[0] :])

    tri = B * len(lower_blocks(n))
    white = pl.pallas_call(
        lambda *refs: factor_kernel(float(total_rows), n, *refs),
        out_shape=jax.ShapeDtypeStruct((tri, B), F32),
        in_specs=[vmem] * 2,
        out_specs=vmem,
        scratch_shapes=[pltpu.VMEM((width, width), F32)],
        compiler_params=params(8),
        cost_estimate=pl.CostEstimate(flops=20_000_000_000, bytes_accessed=8 * tri * B, transcendentals=0),
        name="factor",
    )(cov, extra)
    cxy, white = lax.optimization_barrier((cxy, white))
    cxy_other = gather_end([v[1] for v in cxy], place_other) / total_rows
    cxy = gather_end([v[0] for v in cxy], place) / total_rows
    white_other = shift(white, "gr", 1)

    return pl.pallas_call(
        project_kernel,
        out_shape=(
            jax.ShapeDtypeStruct((rows, width), BF),
            jax.ShapeDtypeStruct((rows, width), BF),
            jax.ShapeDtypeStruct((width, width), F32),
        ),
        in_specs=[smem] + [vmem] * 6,
        out_specs=(hbm,) * 3,
        scratch_shapes=[panel] * 2 + [pltpu.VMEM((width, width), F32)] * 4 + [pltpu.SemaphoreType.DMA((1 + 2 * CHUNKS,))],
        compiler_params=params(24),
        cost_estimate=pl.CostEstimate(flops=8 * rows * width * width, bytes_accessed=16 * rows * width, transcendentals=0),
        name="project",
    )(core_arg, x_states, y_states, white, white_other, cxy, cxy_other)


def solution(mesh):
    return jax.shard_map(
        on_device,
        mesh=mesh,
        in_specs=(P(("gr", "gc"), None), P(("gr", "gc"), None)),
        out_specs=(P(("gr", "gc"), None), P(("gr", "gc"), None), P()),
        check_vma=False,
    )
```

```python
import jax
import jax.numpy as jnp
from jax import lax
from jax.experimental import pallas as pl
from jax.experimental.pallas import tpu as pltpu
from jax.sharding import PartitionSpec as P

RIDGE = 0.1
B = 128
NB = 16
TILE = 8
BF = jnp.bfloat16
F32 = jnp.float32
CHUNKS = 4


def dot(a, b, ca=1, cb=0, precision=None):
    return lax.dot_general(a, b, (((ca,), (cb,)), ((), ())), preferred_element_type=F32, precision=precision)


def dot_f32(a, b, ca=1, cb=0):
    return dot(a, b, ca, cb, lax.Precision.HIGHEST)


def split2(a):
    high = a.astype(BF)
    return high, (a - high.astype(F32)).astype(BF)


def split3(a):
    high = a.astype(BF)
    rest = a - high.astype(F32)
    mid = rest.astype(BF)
    return high, mid, (rest - mid.astype(F32)).astype(BF)


def dot_x3(a, b, ca=1, cb=0):
    ah, al = a
    bh, bl = b
    return dot(jnp.concatenate([ah, ah, al], ca), jnp.concatenate([bh, bl, bh], cb), ca, cb)


def outer_sum(u, v):
    uh, um, ul = split3(u)
    vh, vm, vl = split3(v)
    a = jnp.concatenate([uh, uh, um, uh, ul, um], 0)
    b = jnp.concatenate([vh, vm, vh, vl, vh, vm], 0)
    return dot(a, b, 0, 0)


def inverse_factor(a, beside=()):
    beside = list(beside)
    n = a.shape[0]
    panels = n // NB
    sublane = lax.broadcasted_iota(jnp.int32, (TILE, n), 0)
    lane = lax.broadcasted_iota(jnp.int32, (TILE, n), 1)
    tiles = lambda a: [a[k : k + TILE] for k in range(0, NB, TILE)]
    row = lambda v, k: v[k : k + 1, :]
    now, later, rest = tiles(a[:NB]), tiles(a[NB : 2 * NB]), a[2 * NB :]
    out = []
    for s in range(panels):
        base = NB * s
        groups = now if s == panels - 1 else now + later
        cols = [
            {q: jnp.broadcast_to(v[:, base + q : base + q + 1], (TILE, n)) for q in range(min(NB, TILE * (g + 1)))}
            for g, v in enumerate(groups)
        ]
        inside = (lane >= base) & (lane < base + NB)
        start = lambda g: jnp.where(lane - base - TILE * g == sublane, 1.0, 0.0) if g < len(now) else 0.0
        values = [jnp.where(inside, start(g), v) for g, v in enumerate(groups)]
        pivots = [jnp.ones((TILE, n), F32) for _ in now]
        for k in range(NB):
            tile, sub = divmod(k, TILE)
            d = row(cols[tile][k], sub)
            pivots[tile] = jnp.where(sublane == sub, d, pivots[tile])
            inverse = 1.0 / d
            pivot_row = row(values[tile], sub)
            entries = {q: row(cols[q // TILE][k], q % TILE) for q in range(k + 1, NB)}
            for g in range(tile, len(groups)):
                if g == tile and sub == TILE - 1:
                    continue
                m = cols[g][k] * inverse
                for q in range(k + 1, NB):
                    if q in cols[g]:
                        cols[g][q] = cols[g][q] - m * entries[q]
                if g == tile:
                    m = jnp.where(sublane > sub, m, 0.0)
                values[g] = values[g] - m * pivot_row
        u = jnp.concatenate([v * lax.rsqrt(p) for v, p in zip(values, pivots)], 0)
        out.append(u)
        now = values[len(now) :]
        if s < panels - 2:
            rest = jnp.where(inside[:1], 0.0, rest) - outer_sum(u[:, base + 2 * NB :], u)
            later, rest = tiles(rest[:NB]), rest[NB:]
        if beside:
            beside.pop(0)()
    for work in beside:
        work()
    r = lax.broadcasted_iota(jnp.int32, (n, n), 0)
    c = lax.broadcasted_iota(jnp.int32, (n, n), 1)
    return jnp.where(r >= c, jnp.concatenate(out, 0), 0.0)


def off_diagonal(n):
    return [(i, j) for i in range(n) for j in range(i + 1, n)]


def lower_blocks(n):
    return [(i, j) for i in range(n) for j in range(i + 1)]


def block_iotas():
    return lax.broadcasted_iota(jnp.int32, (B, B), 0), lax.broadcasted_iota(jnp.int32, (B, B), 1)


def folded_rows(n):
    return B * (n // 2 + n * (n - 1) // 2)


def fold(v_ref, o_ref, e_ref):
    n = v_ref.shape[1] // B
    r, c = block_iotas()
    diagonals = []
    for i in range(n):
        g = dot(v_ref[:, B * i : B * (i + 1)], v_ref[:, B * i :], 0, 0)
        diagonals.append(g[:, :B])
        for j in range(i + 1, n):
            k = n // 2 + off_diagonal(n).index((i, j))
            o_ref[B * k : B * (k + 1), :] = g[:, B * (j - i) : B * (j - i + 1)]
    extra = jnp.zeros((TILE, B), F32)
    for p in range(n // 2):
        low, high = diagonals[2 * p], diagonals[2 * p + 1]
        o_ref[B * p : B * (p + 1), :] = jnp.where(r >= c, low, high)
        diagonal = jnp.sum(jnp.where(r == c, high, 0.0), 0, keepdims=True)
        extra = jnp.where(lax.broadcasted_iota(jnp.int32, (TILE, B), 0) == p, diagonal, extra)
    e_ref[...] = jnp.zeros_like(e_ref)
    e_ref[:TILE, :] = extra


def gram_kernel(core_ref, x_ref, y_ref, other_ref, own_ref, gx_ref, ex_ref, gy_ref, ey_ref):
    width = x_ref.shape[1]
    half = width // 2
    core = core_ref[0]
    rows = gx_ref.shape[0]
    fold(x_ref, gx_ref, ex_ref)
    fold(y_ref, gy_ref, ey_ref)

    def write(o_ref, g_ref, e_ref):
        o_ref[:rows, :] = g_ref[...]
        o_ref[o_ref.shape[0] - B :, :] = e_ref[...]

    @pl.when(core == 0)
    def _():
        write(own_ref, gx_ref, ex_ref)
        write(other_ref, gy_ref, ey_ref)

    @pl.when(core == 1)
    def _():
        write(own_ref, gy_ref, ey_ref)
        write(other_ref, gx_ref, ex_ref)

    for owner, o_ref in ((1 - core, other_ref), (core, own_ref)):
        g = dot(x_ref[...], y_ref[:, pl.ds(pl.multiple_of(owner * half, half), half)], 0, 0)
        for j in range(half // B):
            o_ref[rows + width * j : rows + width * (j + 1), :] = g[:, B * j : B * (j + 1)]


def factor_kernel(total_rows, n, s_ref, e_ref, o_ref, f_ref):
    r, c = block_iotas()
    at = lambda i: slice(B * i, B * (i + 1))
    finish = lambda sums: sums / total_rows + jnp.where(r == c, RIDGE, 0.0)
    for p in range(n // 2):
        pair = s_ref[at(p), :]
        turned = pair.T
        f_ref[at(2 * p), at(2 * p)] = finish(jnp.where(r >= c, pair, turned))
        high = jnp.where(r == c, e_ref[p : p + 1, :], jnp.where(r < c, pair, turned))
        f_ref[at(2 * p + 1), at(2 * p + 1)] = finish(high)
    for k, (i, j) in enumerate(off_diagonal(n)):
        f_ref[at(i), at(j)] = s_ref[at(n // 2 + k), :] / total_rows
    beside = []
    a = f_ref[at(0), at(0)]
    for b in range(n):
        w = inverse_factor(a, beside)
        f_ref[at(b), at(b)] = w
        if b == n - 1:
            f_ref[at(b), : B * b] = dot_f32(w, f_ref[at(b), : B * b])
            break
        u = dot_f32(w, f_ref[at(b), at(b + 1)])
        f_ref[at(b), at(b + 1)] = u
        a = f_ref[at(b + 1), at(b + 1)] - dot_f32(u, u, 0, 0)

        def rows(b=b, w=w):
            if b > 0:
                f_ref[at(b), : B * b] = dot_f32(w, f_ref[at(b), : B * b])
            if b + 2 < n:
                f_ref[at(b), B * (b + 2) :] = dot_f32(w, f_ref[at(b), B * (b + 2) :])

        def below(i, b=b, w=w):
            u = f_ref[at(b), at(i)]
            first = B * i if i > b + 1 else B * (i + 1)
            if first < B * n:
                f_ref[at(i), first:] -= dot_f32(u, f_ref[at(b), first:], 0, 0)
            if b > 0:
                f_ref[at(i), : B * b] -= dot_f32(u, f_ref[at(b), : B * b], 0, 0)
            f_ref[at(i), at(b)] = -dot_f32(u, w, 0, 0)

        beside = [rows] + [lambda i=i, below=below: below(i) for i in range(b + 1, n)]
    for k, (i, j) in enumerate(lower_blocks(n)):
        o_ref[at(k), :] = f_ref[at(i), at(j)]


def project_kernel(
    core_ref, x_ref, y_ref, wm_ref, wo_ref, cm_ref, co_ref, px_hbm, py_hbm, cross_hbm,
    px_ref, py_ref, cross_ref, wx_ref, wy_ref, c_ref, sems,
):
    rows, width = x_ref.shape
    n = width // B
    half = width // 2
    core = core_ref[0]
    at = lambda i: slice(B * i, B * (i + 1))

    def unpack(w_x, w_y, c_0, c_1):
        for w_ref, w in ((wx_ref, w_x), (wy_ref, w_y)):
            for i in range(0, n, 2):
                w_ref[at(i), at(i + 1)] = jnp.zeros((B, B), F32)
            for k, (i, j) in enumerate(lower_blocks(n)):
                w_ref[at(i), at(j)] = w[at(k), :]
        for j in range(half // B):
            c_ref[:, at(j)] = c_0[width * j : width * (j + 1), :]
            c_ref[:, half + B * j : half + B * (j + 1)] = c_1[width * j : width * (j + 1), :]

    @pl.when(core == 0)
    def _():
        unpack(wm_ref, wo_ref, cm_ref, co_ref)

    @pl.when(core == 1)
    def _():
        unpack(wo_ref, wm_ref, co_ref, cm_ref)

    ends = range(0, width, 2 * B)
    c_hl = split2(c_ref[...])
    left = []
    for i in ends:
        k = i + 2 * B
        left.append(dot_x3(split2(wx_ref[i:k, :k]), [e[:k] for e in c_hl]))
    left = split2(jnp.concatenate(left, 0))
    for i in ends:
        k = i + 2 * B
        cross_ref[:, i:k] = dot_x3([e[:, :k] for e in left], split2(wy_ref[i:k, :k]), 1, 1)
    copies = [pltpu.make_async_copy(cross_ref, cross_hbm, sems.at[0])]
    copies[0].start()
    cross = split2(cross_ref[...])
    map_x, map_y = [], []
    for i in ends:
        columns = slice(i, i + 2 * B)
        map_x.append(dot_x3(split2(wx_ref[i:, columns]), [e[i:] for e in cross], 0, 0))
        map_y.append(dot_x3([e[:, i:] for e in cross], split2(wy_ref[i:, columns])))
    map_x, map_y = jnp.concatenate(map_x, 0), jnp.concatenate(map_y, 1)
    step = rows // CHUNKS
    for ref, p_ref, p_hbm, m, cb in ((x_ref, px_ref, px_hbm, map_x, 0), (y_ref, py_ref, py_hbm, map_y, 1)):
        m = jnp.concatenate(split2(m), cb)
        for k in range(CHUNKS):
            part = pl.ds(k * step, step)
            v = ref[part, :]
            p_ref[part, :] = dot(jnp.concatenate([v, v], 1), m, 1, cb).astype(BF)
            copies.append(pltpu.make_async_copy(p_ref.at[part], p_hbm.at[part], sems.at[len(copies)]))
            copies[-1].start()
    for copy in copies:
        copy.wait()


def params(mib):
    return pltpu.CompilerParams(vmem_limit_bytes=mib * 1024 * 1024)


def shift(v, axis, m):
    return lax.ppermute(v, axis, [(i, i ^ m) for i in range(lax.axis_size(axis))])


def scatter_start(v, axis, n, step, index):
    rows = v.shape[0] // n
    block = lambda k: lax.dynamic_slice_in_dim(v, k * rows, rows, 0)
    return block(index), [shift(block(index ^ m), axis, m * step) for m in range(1, n)]


def scatter_end(state):
    total, parts = state
    for part in parts:
        total = total + part
    return total


def gather_start(v, axis, n, step):
    return [v] + [shift(v, axis, m * step) for m in range(1, n)]


def gather_end(parts, place):
    stacked = jnp.stack(parts)
    return jnp.concatenate([lax.dynamic_index_in_dim(stacked, p, 0, keepdims=False) for p in place], 0)


def plane_scatter(v, chips, core, chip):
    bits = chips.bit_length() - 1
    for s in range(bits):
        masks = 1 << s, 1 << (bits - 1 - s)
        mask = jnp.where(core == 0, *masks)
        bit = (chip & mask) // mask
        rows = v.shape[0] // 2
        half = lambda k: lax.dynamic_slice_in_dim(v, k * rows, rows, 0)
        pairs = [(i, i ^ (2 * masks[i % 2])) for i in range(2 * chips)]
        v = half(bit) + lax.ppermute(half(1 - bit), "gr", pairs)
    reverse = lambda k: sum(((k >> b) & 1) << (bits - 1 - b) for b in range(bits))
    return v, [(k, reverse(k)) for k in range(chips)]


def on_device(x_states, y_states):
    rows, width = x_states.shape
    n = width // B
    gr, gc = lax.axis_size("gr"), lax.axis_size("gc")
    chips = gr // 2
    total_rows = rows * gr * gc
    core = lax.axis_index("gr") % 2
    chip = lax.axis_index("gr") // 2
    plane = lax.axis_index("gc")
    core_arg = jnp.reshape(core, (1,)).astype(jnp.int32)
    smem = pl.BlockSpec(memory_space=pltpu.SMEM)
    vmem = pl.BlockSpec(memory_space=pltpu.VMEM)
    hbm = pl.BlockSpec(memory_space=pltpu.HBM)
    folded = folded_rows(n)
    half = width * width // 2 // B
    panel = pltpu.VMEM((rows, width), BF)
    gram = pltpu.VMEM((folded, B), F32)
    extra = pltpu.VMEM((B, B), F32)
    packed = jax.ShapeDtypeStruct((folded + half + B, B), F32)

    other, own = pl.pallas_call(
        gram_kernel,
        out_shape=(packed,) * 2,
        in_specs=[smem, vmem, vmem],
        out_specs=(vmem,) * 2,
        scratch_shapes=[gram, extra] * 2,
        compiler_params=params(10),
        cost_estimate=pl.CostEstimate(flops=4 * rows * (folded + half) * B, bytes_accessed=8 * rows * width, transcendentals=0),
        name="gram",
    )(core_arg, x_states, y_states)
    sums = own + shift(other, "gr", 1)
    shards = chips * gc
    blocks = lambda v: jnp.reshape(v, (shards, -1, B))
    flat = lambda v: jnp.reshape(v, (-1, B))
    parts = sums[:folded], sums[folded + half :], sums[folded : folded + half]
    sums = flat(jnp.concatenate([blocks(v) for v in parts], 1))
    sums, place = plane_scatter(sums, chips, core, chip)
    place = [chip ^ jnp.where(core == 0, b, a) for a, b in place]
    sums = scatter_end(scatter_start(sums, "gc", gc, 1, plane))
    sums = gather_end(gather_start(sums, "gc", gc, 1), [plane ^ k for k in range(gc)])
    sums = jnp.reshape(sums, (gc, -1, B))
    sizes = folded // shards, (folded + B) // shards
    cov = gather_start(flat(sums[:, : sizes[1]]), "gr", chips, 2)
    cxy = gather_start(flat(sums[:, sizes[1] :]), "gr", chips, 2)
    cov = jnp.reshape(gather_end(cov, place), (shards, -1, B))
    cov, extra = flat(cov[:, : sizes[0]]), flat(cov[:, sizes[0] :])

    tri = B * len(lower_blocks(n))
    white = pl.pallas_call(
        lambda *refs: factor_kernel(float(total_rows), n, *refs),
        out_shape=jax.ShapeDtypeStruct((tri, B), F32),
        in_specs=[vmem] * 2,
        out_specs=vmem,
        scratch_shapes=[pltpu.VMEM((width, width), F32)],
        compiler_params=params(8),
        cost_estimate=pl.CostEstimate(flops=20_000_000_000, bytes_accessed=8 * tri * B, transcendentals=0),
        name="factor",
    )(cov, extra)
    cxy, white = lax.optimization_barrier((cxy, white))
    cxy = gather_end(cxy, place) / total_rows
    cxy_other = shift(cxy, "gr", 1)
    white_other = shift(white, "gr", 1)

    return pl.pallas_call(
        project_kernel,
        out_shape=(
            jax.ShapeDtypeStruct((rows, width), BF),
            jax.ShapeDtypeStruct((rows, width), BF),
            jax.ShapeDtypeStruct((width, width), F32),
        ),
        in_specs=[smem] + [vmem] * 6,
        out_specs=(hbm,) * 3,
        scratch_shapes=[panel] * 2 + [pltpu.VMEM((width, width), F32)] * 4 + [pltpu.SemaphoreType.DMA((1 + 2 * CHUNKS,))],
        compiler_params=params(24),
        cost_estimate=pl.CostEstimate(flops=8 * rows * width * width, bytes_accessed=16 * rows * width, transcendentals=0),
        name="project",
    )(core_arg, x_states, y_states, white, white_other, cxy, cxy_other)


def solution(mesh):
    return jax.shard_map(
        on_device,
        mesh=mesh,
        in_specs=(P(("gr", "gc"), None), P(("gr", "gc"), None)),
        out_specs=(P(("gr", "gc"), None), P(("gr", "gc"), None), P()),
        check_vma=False,
    )
```

```python
import jax
import jax.numpy as jnp
from jax import lax
from jax.experimental import pallas as pl
from jax.experimental.pallas import tpu as pltpu
from jax.sharding import PartitionSpec as P

RIDGE = 0.1
B = 128
NB = 16
TILE = 8
BF = jnp.bfloat16
F32 = jnp.float32
CHUNKS = 4


def dot(a, b, ca=1, cb=0, precision=None):
    return lax.dot_general(a, b, (((ca,), (cb,)), ((), ())), preferred_element_type=F32, precision=precision)


def dot_f32(a, b, ca=1, cb=0):
    return dot(a, b, ca, cb, lax.Precision.HIGHEST)


def split2(a):
    high = a.astype(BF)
    return high, (a - high.astype(F32)).astype(BF)


def split3(a):
    high = a.astype(BF)
    rest = a - high.astype(F32)
    mid = rest.astype(BF)
    return high, mid, (rest - mid.astype(F32)).astype(BF)


def dot_x3(a, b, ca=1, cb=0):
    ah, al = a
    bh, bl = b
    return dot(jnp.concatenate([ah, ah, al], ca), jnp.concatenate([bh, bl, bh], cb), ca, cb)


def outer_sum(u, v):
    uh, um, ul = split3(u)
    vh, vm, vl = split3(v)
    a = jnp.concatenate([uh, uh, um, uh, ul, um], 0)
    b = jnp.concatenate([vh, vm, vh, vl, vh, vm], 0)
    return dot(a, b, 0, 0)


def inverse_factor(a, beside=()):
    beside = list(beside)
    n = a.shape[0]
    panels = n // NB
    sublane = lax.broadcasted_iota(jnp.int32, (TILE, n), 0)
    lane = lax.broadcasted_iota(jnp.int32, (TILE, n), 1)
    tiles = lambda a: [a[k : k + TILE] for k in range(0, NB, TILE)]
    row = lambda v, k: v[k : k + 1, :]
    now, later, rest = tiles(a[:NB]), tiles(a[NB : 2 * NB]), a[2 * NB :]
    out = []
    for s in range(panels):
        base = NB * s
        groups = now if s == panels - 1 else now + later
        cols = [
            {q: jnp.broadcast_to(v[:, base + q : base + q + 1], (TILE, n)) for q in range(min(NB, TILE * (g + 1)))}
            for g, v in enumerate(groups)
        ]
        inside = (lane >= base) & (lane < base + NB)
        start = lambda g: jnp.where(lane - base - TILE * g == sublane, 1.0, 0.0) if g < len(now) else 0.0
        values = [jnp.where(inside, start(g), v) for g, v in enumerate(groups)]
        pivots = [jnp.ones((TILE, n), F32) for _ in now]
        for k in range(NB):
            tile, sub = divmod(k, TILE)
            d = row(cols[tile][k], sub)
            pivots[tile] = jnp.where(sublane == sub, d, pivots[tile])
            inverse = 1.0 / d
            pivot_row = row(values[tile], sub)
            entries = {q: row(cols[q // TILE][k], q % TILE) for q in range(k + 1, NB)}
            for g in range(tile, len(groups)):
                if g == tile and sub == TILE - 1:
                    continue
                m = cols[g][k] * inverse
                for q in range(k + 1, NB):
                    if q in cols[g]:
                        cols[g][q] = cols[g][q] - m * entries[q]
                if g == tile:
                    m = jnp.where(sublane > sub, m, 0.0)
                values[g] = values[g] - m * pivot_row
        u = jnp.concatenate([v * lax.rsqrt(p) for v, p in zip(values, pivots)], 0)
        out.append(u)
        now = values[len(now) :]
        if s < panels - 2:
            rest = jnp.where(inside[:1], 0.0, rest) - outer_sum(u[:, base + 2 * NB :], u)
            later, rest = tiles(rest[:NB]), rest[NB:]
        if beside:
            beside.pop(0)()
    for work in beside:
        work()
    r = lax.broadcasted_iota(jnp.int32, (n, n), 0)
    c = lax.broadcasted_iota(jnp.int32, (n, n), 1)
    return jnp.where(r >= c, jnp.concatenate(out, 0), 0.0)


def off_diagonal(n):
    return [(i, j) for i in range(n) for j in range(i + 1, n)]


def lower_blocks(n):
    return [(i, j) for i in range(n) for j in range(i + 1)]


def block_iotas():
    return lax.broadcasted_iota(jnp.int32, (B, B), 0), lax.broadcasted_iota(jnp.int32, (B, B), 1)


def folded_rows(n):
    return B * (n // 2 + n * (n - 1) // 2)


def fold(v_ref, o_ref, e_ref):
    n = v_ref.shape[1] // B
    r, c = block_iotas()
    diagonals = []
    for i in range(n):
        g = dot(v_ref[:, B * i : B * (i + 1)], v_ref[:, B * i :], 0, 0)
        diagonals.append(g[:, :B])
        for j in range(i + 1, n):
            k = n // 2 + off_diagonal(n).index((i, j))
            o_ref[B * k : B * (k + 1), :] = g[:, B * (j - i) : B * (j - i + 1)]
    extra = jnp.zeros((TILE, B), F32)
    for p in range(n // 2):
        low, high = diagonals[2 * p], diagonals[2 * p + 1]
        o_ref[B * p : B * (p + 1), :] = jnp.where(r >= c, low, high)
        diagonal = jnp.sum(jnp.where(r == c, high, 0.0), 0, keepdims=True)
        extra = jnp.where(lax.broadcasted_iota(jnp.int32, (TILE, B), 0) == p, diagonal, extra)
    e_ref[...] = jnp.zeros_like(e_ref)
    e_ref[:TILE, :] = extra


def gram_kernel(core_ref, x_ref, y_ref, other_ref, own_ref, gx_ref, ex_ref, gy_ref, ey_ref):
    width = x_ref.shape[1]
    half = width // 2
    core = core_ref[0]
    rows = gx_ref.shape[0]
    fold(x_ref, gx_ref, ex_ref)
    fold(y_ref, gy_ref, ey_ref)

    cxy = dot(x_ref[...], y_ref[...], 0, 0)

    def write(o_ref, g_ref, e_ref, first):
        o_ref[:rows, :] = g_ref[...]
        o_ref[o_ref.shape[0] - B :, :] = e_ref[...]
        for j in range(half // B):
            o_ref[rows + width * j : rows + width * (j + 1), :] = cxy[:, first + B * j : first + B * (j + 1)]

    @pl.when(core == 0)
    def _():
        write(own_ref, gx_ref, ex_ref, 0)
        write(other_ref, gy_ref, ey_ref, half)

    @pl.when(core == 1)
    def _():
        write(own_ref, gy_ref, ey_ref, half)
        write(other_ref, gx_ref, ex_ref, 0)


def factor_kernel(total_rows, n, s_ref, e_ref, o_ref, f_ref):
    r, c = block_iotas()
    at = lambda i: slice(B * i, B * (i + 1))
    finish = lambda sums: sums / total_rows + jnp.where(r == c, RIDGE, 0.0)
    for p in range(n // 2):
        pair = s_ref[at(p), :]
        turned = pair.T
        f_ref[at(2 * p), at(2 * p)] = finish(jnp.where(r >= c, pair, turned))
        high = jnp.where(r == c, e_ref[p : p + 1, :], jnp.where(r < c, pair, turned))
        f_ref[at(2 * p + 1), at(2 * p + 1)] = finish(high)
    for k, (i, j) in enumerate(off_diagonal(n)):
        f_ref[at(i), at(j)] = s_ref[at(n // 2 + k), :] / total_rows
    beside = []
    a = f_ref[at(0), at(0)]
    for b in range(n):
        w = inverse_factor(a, beside)
        f_ref[at(b), at(b)] = w
        if b == n - 1:
            f_ref[at(b), : B * b] = dot_f32(w, f_ref[at(b), : B * b])
            break
        u = dot_f32(w, f_ref[at(b), at(b + 1)])
        f_ref[at(b), at(b + 1)] = u
        a = f_ref[at(b + 1), at(b + 1)] - dot_f32(u, u, 0, 0)

        def rows(b=b, w=w):
            if b > 0:
                f_ref[at(b), : B * b] = dot_f32(w, f_ref[at(b), : B * b])
            if b + 2 < n:
                f_ref[at(b), B * (b + 2) :] = dot_f32(w, f_ref[at(b), B * (b + 2) :])

        def below(i, b=b, w=w):
            u = f_ref[at(b), at(i)]
            first = B * i if i > b + 1 else B * (i + 1)
            if first < B * n:
                f_ref[at(i), first:] -= dot_f32(u, f_ref[at(b), first:], 0, 0)
            if b > 0:
                f_ref[at(i), : B * b] -= dot_f32(u, f_ref[at(b), : B * b], 0, 0)
            f_ref[at(i), at(b)] = -dot_f32(u, w, 0, 0)

        beside = [rows] + [lambda i=i, below=below: below(i) for i in range(b + 1, n)]
    for k, (i, j) in enumerate(lower_blocks(n)):
        o_ref[at(k), :] = f_ref[at(i), at(j)]


def project_kernel(
    core_ref, x_ref, y_ref, wm_ref, wo_ref, cm_ref, co_ref, px_hbm, py_hbm, cross_hbm,
    px_ref, py_ref, cross_ref, wx_ref, wy_ref, c_ref, sems,
):
    rows, width = x_ref.shape
    n = width // B
    half = width // 2
    core = core_ref[0]
    at = lambda i: slice(B * i, B * (i + 1))

    def unpack(w_x, w_y, c_0, c_1):
        for w_ref, w in ((wx_ref, w_x), (wy_ref, w_y)):
            for i in range(0, n, 2):
                w_ref[at(i), at(i + 1)] = jnp.zeros((B, B), F32)
            for k, (i, j) in enumerate(lower_blocks(n)):
                w_ref[at(i), at(j)] = w[at(k), :]
        for j in range(half // B):
            c_ref[:, at(j)] = c_0[width * j : width * (j + 1), :]
            c_ref[:, half + B * j : half + B * (j + 1)] = c_1[width * j : width * (j + 1), :]

    @pl.when(core == 0)
    def _():
        unpack(wm_ref, wo_ref, cm_ref, co_ref)

    @pl.when(core == 1)
    def _():
        unpack(wo_ref, wm_ref, co_ref, cm_ref)

    ends = range(0, width, 2 * B)
    left = []
    for i in ends:
        k = i + 2 * B
        left.append(dot_f32(wx_ref[i:k, :k], c_ref[:k, :]))
    left = split2(jnp.concatenate(left, 0))
    for i in ends:
        k = i + 2 * B
        cross_ref[:, i:k] = dot_x3([e[:, :k] for e in left], split2(wy_ref[i:k, :k]), 1, 1)
    copies = [pltpu.make_async_copy(cross_ref, cross_hbm, sems.at[0])]
    copies[0].start()
    cross = split2(cross_ref[...])
    map_x, map_y = [], []
    for i in ends:
        columns = slice(i, i + 2 * B)
        map_x.append(dot_x3(split2(wx_ref[i:, columns]), [e[i:] for e in cross], 0, 0))
        map_y.append(dot_x3([e[:, i:] for e in cross], split2(wy_ref[i:, columns])))
    map_x, map_y = jnp.concatenate(map_x, 0), jnp.concatenate(map_y, 1)
    step = rows // CHUNKS
    for ref, p_ref, p_hbm, m, cb in ((x_ref, px_ref, px_hbm, map_x, 0), (y_ref, py_ref, py_hbm, map_y, 1)):
        m = jnp.concatenate(split2(m), cb)
        for k in range(CHUNKS):
            part = pl.ds(k * step, step)
            v = ref[part, :]
            p_ref[part, :] = dot(jnp.concatenate([v, v], 1), m, 1, cb).astype(BF)
            copies.append(pltpu.make_async_copy(p_ref.at[part], p_hbm.at[part], sems.at[len(copies)]))
            copies[-1].start()
    for copy in copies:
        copy.wait()


def params(mib):
    return pltpu.CompilerParams(vmem_limit_bytes=mib * 1024 * 1024)


def shift(v, axis, m):
    return lax.ppermute(v, axis, [(i, i ^ m) for i in range(lax.axis_size(axis))])


def scatter_start(v, axis, n, step, index):
    rows = v.shape[0] // n
    block = lambda k: lax.dynamic_slice_in_dim(v, k * rows, rows, 0)
    return block(index), [shift(block(index ^ m), axis, m * step) for m in range(1, n)]


def scatter_end(state):
    total, parts = state
    for part in parts:
        total = total + part
    return total


def gather_start(v, axis, n, step):
    return [v] + [shift(v, axis, m * step) for m in range(1, n)]


def gather_end(parts, place):
    stacked = jnp.stack(parts)
    return jnp.concatenate([lax.dynamic_index_in_dim(stacked, p, 0, keepdims=False) for p in place], 0)


def plane_scatter(v, chips, core, chip):
    bits = chips.bit_length() - 1
    for s in range(bits):
        masks = 1 << (bits - 1 - s), 1 << s
        mask = jnp.where(core == 0, *masks)
        bit = (chip & mask) // mask
        rows = v.shape[0] // 2
        half = lambda k: lax.dynamic_slice_in_dim(v, k * rows, rows, 0)
        pairs = [(i, i ^ (2 * masks[i % 2])) for i in range(2 * chips)]
        v = half(bit) + lax.ppermute(half(1 - bit), "gr", pairs)
    reverse = lambda k: sum(((k >> b) & 1) << (bits - 1 - b) for b in range(bits))
    return v, [(reverse(k), k) for k in range(chips)]


def on_device(x_states, y_states):
    rows, width = x_states.shape
    n = width // B
    gr, gc = lax.axis_size("gr"), lax.axis_size("gc")
    chips = gr // 2
    total_rows = rows * gr * gc
    core = lax.axis_index("gr") % 2
    chip = lax.axis_index("gr") // 2
    plane = lax.axis_index("gc")
    core_arg = jnp.reshape(core, (1,)).astype(jnp.int32)
    smem = pl.BlockSpec(memory_space=pltpu.SMEM)
    vmem = pl.BlockSpec(memory_space=pltpu.VMEM)
    hbm = pl.BlockSpec(memory_space=pltpu.HBM)
    folded = folded_rows(n)
    half = width * width // 2 // B
    panel = pltpu.VMEM((rows, width), BF)
    gram = pltpu.VMEM((folded, B), F32)
    extra = pltpu.VMEM((B, B), F32)
    packed = jax.ShapeDtypeStruct((folded + half + B, B), F32)

    other, own = pl.pallas_call(
        gram_kernel,
        out_shape=(packed,) * 2,
        in_specs=[smem, vmem, vmem],
        out_specs=(vmem,) * 2,
        scratch_shapes=[gram, extra] * 2,
        compiler_params=params(10),
        cost_estimate=pl.CostEstimate(flops=4 * rows * (folded + half) * B, bytes_accessed=8 * rows * width, transcendentals=0),
        name="gram",
    )(core_arg, x_states, y_states)
    sums = own + shift(other, "gr", 1)
    shards = chips * gc
    blocks = lambda v: jnp.reshape(v, (shards, -1, B))
    flat = lambda v: jnp.reshape(v, (-1, B))
    parts = sums[:folded], sums[folded + half :], sums[folded : folded + half]
    sums = flat(jnp.concatenate([blocks(v) for v in parts], 1))
    sums, place = plane_scatter(sums, chips, core, chip)
    place = [chip ^ jnp.where(core == 0, b, a) for a, b in place]
    sums = scatter_end(scatter_start(sums, "gc", gc, 1, plane))
    sums = gather_end(gather_start(sums, "gc", gc, 1), [plane ^ k for k in range(gc)])
    sums = jnp.reshape(sums, (gc, -1, B))
    sizes = folded // shards, (folded + B) // shards
    cov = gather_start(flat(sums[:, : sizes[1]]), "gr", chips, 2)
    cxy = gather_start(flat(sums[:, sizes[1] :]), "gr", chips, 2)
    cov = jnp.reshape(gather_end(cov, place), (shards, -1, B))
    cov, extra = flat(cov[:, : sizes[0]]), flat(cov[:, sizes[0] :])

    tri = B * len(lower_blocks(n))
    white = pl.pallas_call(
        lambda *refs: factor_kernel(float(total_rows), n, *refs),
        out_shape=jax.ShapeDtypeStruct((tri, B), F32),
        in_specs=[vmem] * 2,
        out_specs=vmem,
        scratch_shapes=[pltpu.VMEM((width, width), F32)],
        compiler_params=params(8),
        cost_estimate=pl.CostEstimate(flops=20_000_000_000, bytes_accessed=8 * tri * B, transcendentals=0),
        name="factor",
    )(cov, extra)
    cxy, white = lax.optimization_barrier((cxy, white))
    cxy = gather_end(cxy, place) / total_rows
    cxy_other = shift(cxy, "gr", 1)
    white_other = shift(white, "gr", 1)

    return pl.pallas_call(
        project_kernel,
        out_shape=(
            jax.ShapeDtypeStruct((rows, width), BF),
            jax.ShapeDtypeStruct((rows, width), BF),
            jax.ShapeDtypeStruct((width, width), F32),
        ),
        in_specs=[smem] + [vmem] * 6,
        out_specs=(hbm,) * 3,
        scratch_shapes=[panel] * 2 + [pltpu.VMEM((width, width), F32)] * 4 + [pltpu.SemaphoreType.DMA((1 + 2 * CHUNKS,))],
        compiler_params=params(24),
        cost_estimate=pl.CostEstimate(flops=8 * rows * width * width, bytes_accessed=16 * rows * width, transcendentals=0),
        name="project",
    )(core_arg, x_states, y_states, white, white_other, cxy, cxy_other)


def solution(mesh):
    return jax.shard_map(
        on_device,
        mesh=mesh,
        in_specs=(P(("gr", "gc"), None), P(("gr", "gc"), None)),
        out_specs=(P(("gr", "gc"), None), P(("gr", "gc"), None), P()),
        check_vma=False,
    )
```

```python
import jax
import jax.numpy as jnp
from jax import lax
from jax.experimental import pallas as pl
from jax.experimental.pallas import tpu as pltpu
from jax.sharding import PartitionSpec as P

RIDGE = 0.1
B = 128
NB = 16
TILE = 8
BF = jnp.bfloat16
F32 = jnp.float32
CHUNKS = 4


def dot(a, b, ca=1, cb=0, precision=None):
    return lax.dot_general(a, b, (((ca,), (cb,)), ((), ())), preferred_element_type=F32, precision=precision)


def dot_f32(a, b, ca=1, cb=0):
    return dot(a, b, ca, cb, lax.Precision.HIGHEST)


def split2(a):
    high = a.astype(BF)
    return high, (a - high.astype(F32)).astype(BF)


def split3(a):
    high = a.astype(BF)
    rest = a - high.astype(F32)
    mid = rest.astype(BF)
    return high, mid, (rest - mid.astype(F32)).astype(BF)


def dot_x3(a, b, ca=1, cb=0):
    ah, al = a
    bh, bl = b
    return dot(jnp.concatenate([ah, ah, al], ca), jnp.concatenate([bh, bl, bh], cb), ca, cb)


def outer_sum(u, v):
    uh, um, ul = split3(u)
    vh, vm, vl = split3(v)
    a = jnp.concatenate([uh, uh, um, uh, ul, um], 0)
    b = jnp.concatenate([vh, vm, vh, vl, vh, vm], 0)
    return dot(a, b, 0, 0)


def inverse_factor(a, beside=()):
    beside = list(beside)
    n = a.shape[0]
    panels = n // NB
    sublane = lax.broadcasted_iota(jnp.int32, (TILE, n), 0)
    lane = lax.broadcasted_iota(jnp.int32, (TILE, n), 1)
    tiles = lambda a: [a[k : k + TILE] for k in range(0, NB, TILE)]
    row = lambda v, k: v[k : k + 1, :]
    now, later, rest = tiles(a[:NB]), tiles(a[NB : 2 * NB]), a[2 * NB :]
    out = []
    for s in range(panels):
        base = NB * s
        groups = now if s == panels - 1 else now + later
        cols = [
            {q: jnp.broadcast_to(v[:, base + q : base + q + 1], (TILE, n)) for q in range(min(NB, TILE * (g + 1)))}
            for g, v in enumerate(groups)
        ]
        inside = (lane >= base) & (lane < base + NB)
        start = lambda g: jnp.where(lane - base - TILE * g == sublane, 1.0, 0.0) if g < len(now) else 0.0
        values = [jnp.where(inside, start(g), v) for g, v in enumerate(groups)]
        pivots = [jnp.ones((TILE, n), F32) for _ in now]
        for k in range(NB):
            tile, sub = divmod(k, TILE)
            d = row(cols[tile][k], sub)
            pivots[tile] = jnp.where(sublane == sub, d, pivots[tile])
            inverse = 1.0 / d
            pivot_row = row(values[tile], sub)
            entries = {q: row(cols[q // TILE][k], q % TILE) for q in range(k + 1, NB)}
            for g in range(tile, len(groups)):
                if g == tile and sub == TILE - 1:
                    continue
                m = cols[g][k] * inverse
                for q in range(k + 1, NB):
                    if q in cols[g]:
                        cols[g][q] = cols[g][q] - m * entries[q]
                if g == tile:
                    m = jnp.where(sublane > sub, m, 0.0)
                values[g] = values[g] - m * pivot_row
        u = jnp.concatenate([v * lax.rsqrt(p) for v, p in zip(values, pivots)], 0)
        out.append(u)
        now = values[len(now) :]
        if s < panels - 2:
            rest = jnp.where(inside[:1], 0.0, rest) - outer_sum(u[:, base + 2 * NB :], u)
            later, rest = tiles(rest[:NB]), rest[NB:]
        if beside:
            beside.pop(0)()
    for work in beside:
        work()
    r = lax.broadcasted_iota(jnp.int32, (n, n), 0)
    c = lax.broadcasted_iota(jnp.int32, (n, n), 1)
    return jnp.where(r >= c, jnp.concatenate(out, 0), 0.0)


def off_diagonal(n):
    return [(i, j) for i in range(n) for j in range(i + 1, n)]


def lower_blocks(n):
    return [(i, j) for i in range(n) for j in range(i + 1)]


def block_iotas():
    return lax.broadcasted_iota(jnp.int32, (B, B), 0), lax.broadcasted_iota(jnp.int32, (B, B), 1)


def folded_rows(n):
    return B * (n // 2 + n * (n - 1) // 2)


def fold(v_ref, o_ref, e_ref):
    n = v_ref.shape[1] // B
    r, c = block_iotas()
    diagonals = []
    for i in range(n):
        g = dot(v_ref[:, B * i : B * (i + 1)], v_ref[:, B * i :], 0, 0)
        diagonals.append(g[:, :B])
        for j in range(i + 1, n):
            k = n // 2 + off_diagonal(n).index((i, j))
            o_ref[B * k : B * (k + 1), :] = g[:, B * (j - i) : B * (j - i + 1)]
    extra = jnp.zeros((TILE, B), F32)
    for p in range(n // 2):
        low, high = diagonals[2 * p], diagonals[2 * p + 1]
        o_ref[B * p : B * (p + 1), :] = jnp.where(r >= c, low, high)
        diagonal = jnp.sum(jnp.where(r == c, high, 0.0), 0, keepdims=True)
        extra = jnp.where(lax.broadcasted_iota(jnp.int32, (TILE, B), 0) == p, diagonal, extra)
    e_ref[...] = jnp.zeros_like(e_ref)
    e_ref[:TILE, :] = extra


def gram_kernel(core_ref, x_ref, y_ref, other_ref, own_ref, gx_ref, ex_ref, gy_ref, ey_ref):
    width = x_ref.shape[1]
    half = width // 2
    core = core_ref[0]
    rows = gx_ref.shape[0]
    fold(x_ref, gx_ref, ex_ref)
    fold(y_ref, gy_ref, ey_ref)

    cxy = dot(x_ref[...], y_ref[...], 0, 0)

    def write(o_ref, g_ref, e_ref, first):
        o_ref[:rows, :] = g_ref[...]
        o_ref[o_ref.shape[0] - B :, :] = e_ref[...]
        for j in range(half // B):
            o_ref[rows + width * j : rows + width * (j + 1), :] = cxy[:, first + B * j : first + B * (j + 1)]

    @pl.when(core == 0)
    def _():
        write(own_ref, gx_ref, ex_ref, 0)
        write(other_ref, gy_ref, ey_ref, half)

    @pl.when(core == 1)
    def _():
        write(own_ref, gy_ref, ey_ref, half)
        write(other_ref, gx_ref, ex_ref, 0)


def factor_kernel(total_rows, n, shards, s_ref, o_ref, f_ref):
    r, c = block_iotas()
    at = lambda i: slice(B * i, B * (i + 1))
    own, more = folded_rows(n) // shards, B // shards
    finish = lambda sums: sums / total_rows + jnp.where(r == c, RIDGE, 0.0)

    def block(k):
        starts = [(own + more) * (B * k // own + i) for i in range(B // own)]
        return jnp.concatenate([s_ref[i : i + own, :] for i in starts], 0)

    for p in range(n // 2):
        pair = block(p)
        turned = pair.T
        f_ref[at(2 * p), at(2 * p)] = finish(jnp.where(r >= c, pair, turned))
        extra = (own + more) * (p // more) + own + p % more
        high = jnp.where(r == c, s_ref[extra : extra + 1, :], jnp.where(r < c, pair, turned))
        f_ref[at(2 * p + 1), at(2 * p + 1)] = finish(high)
    for k, (i, j) in enumerate(off_diagonal(n)):
        f_ref[at(i), at(j)] = block(n // 2 + k) / total_rows
    beside = []
    a = f_ref[at(0), at(0)]
    for b in range(n):
        w = inverse_factor(a, beside)
        f_ref[at(b), at(b)] = w
        if b == n - 1:
            f_ref[at(b), : B * b] = dot_f32(w, f_ref[at(b), : B * b])
            break
        u = dot_f32(w, f_ref[at(b), at(b + 1)])
        f_ref[at(b), at(b + 1)] = u
        a = f_ref[at(b + 1), at(b + 1)] - dot_f32(u, u, 0, 0)

        def rows(b=b, w=w):
            if b > 0:
                f_ref[at(b), : B * b] = dot_f32(w, f_ref[at(b), : B * b])
            if b + 2 < n:
                f_ref[at(b), B * (b + 2) :] = dot_f32(w, f_ref[at(b), B * (b + 2) :])

        def below(i, b=b, w=w):
            u = f_ref[at(b), at(i)]
            first = B * i if i > b + 1 else B * (i + 1)
            if first < B * n:
                f_ref[at(i), first:] -= dot_f32(u, f_ref[at(b), first:], 0, 0)
            if b > 0:
                f_ref[at(i), : B * b] -= dot_f32(u, f_ref[at(b), : B * b], 0, 0)
            f_ref[at(i), at(b)] = -dot_f32(u, w, 0, 0)

        beside = [rows] + [lambda i=i, below=below: below(i) for i in range(b + 1, n)]
    for k, (i, j) in enumerate(lower_blocks(n)):
        o_ref[at(k), :] = f_ref[at(i), at(j)]


def project_kernel(
    core_ref, x_ref, y_ref, wm_ref, wo_ref, cm_ref, co_ref, px_hbm, py_hbm, cross_hbm,
    px_ref, py_ref, cross_ref, wx_ref, wy_ref, c_ref, sems,
):
    rows, width = x_ref.shape
    n = width // B
    half = width // 2
    core = core_ref[0]
    at = lambda i: slice(B * i, B * (i + 1))

    def unpack(w_x, w_y, c_0, c_1):
        for w_ref, w in ((wx_ref, w_x), (wy_ref, w_y)):
            for i in range(0, n, 2):
                w_ref[at(i), at(i + 1)] = jnp.zeros((B, B), F32)
            for k, (i, j) in enumerate(lower_blocks(n)):
                w_ref[at(i), at(j)] = w[at(k), :]
        for j in range(half // B):
            c_ref[:, at(j)] = c_0[width * j : width * (j + 1), :]
            c_ref[:, half + B * j : half + B * (j + 1)] = c_1[width * j : width * (j + 1), :]

    @pl.when(core == 0)
    def _():
        unpack(wm_ref, wo_ref, cm_ref, co_ref)

    @pl.when(core == 1)
    def _():
        unpack(wo_ref, wm_ref, co_ref, cm_ref)

    ends = range(0, width, 2 * B)
    left = []
    for i in ends:
        k = i + 2 * B
        left.append(dot_f32(wx_ref[i:k, :k], c_ref[:k, :]))
    left = split2(jnp.concatenate(left, 0))
    for i in ends:
        k = i + 2 * B
        cross_ref[:, i:k] = dot_x3([e[:, :k] for e in left], split2(wy_ref[i:k, :k]), 1, 1)
    copies = [pltpu.make_async_copy(cross_ref, cross_hbm, sems.at[0])]
    copies[0].start()
    cross = split2(cross_ref[...])
    map_x, map_y = [], []
    for i in ends:
        columns = slice(i, i + 2 * B)
        map_x.append(dot_x3(split2(wx_ref[i:, columns]), [e[i:] for e in cross], 0, 0))
        map_y.append(dot_x3([e[:, i:] for e in cross], split2(wy_ref[i:, columns])))
    map_x, map_y = jnp.concatenate(map_x, 0), jnp.concatenate(map_y, 1)
    step = rows // CHUNKS
    for ref, p_ref, p_hbm, m, cb in ((x_ref, px_ref, px_hbm, map_x, 0), (y_ref, py_ref, py_hbm, map_y, 1)):
        m = jnp.concatenate(split2(m), cb)
        for k in range(CHUNKS):
            part = pl.ds(k * step, step)
            v = ref[part, :]
            p_ref[part, :] = dot(jnp.concatenate([v, v], 1), m, 1, cb).astype(BF)
            copies.append(pltpu.make_async_copy(p_ref.at[part], p_hbm.at[part], sems.at[len(copies)]))
            copies[-1].start()
    for copy in copies:
        copy.wait()


def params(mib):
    return pltpu.CompilerParams(vmem_limit_bytes=mib * 1024 * 1024)


def shift(v, axis, m):
    return lax.ppermute(v, axis, [(i, i ^ m) for i in range(lax.axis_size(axis))])


def scatter_start(v, axis, n, step, index):
    rows = v.shape[0] // n
    block = lambda k: lax.dynamic_slice_in_dim(v, k * rows, rows, 0)
    return block(index), [shift(block(index ^ m), axis, m * step) for m in range(1, n)]


def scatter_end(state):
    total, parts = state
    for part in parts:
        total = total + part
    return total


def gather_start(v, axis, n, step):
    return [v] + [shift(v, axis, m * step) for m in range(1, n)]


def gather_end(parts, place):
    stacked = jnp.stack(parts)
    return jnp.concatenate([lax.dynamic_index_in_dim(stacked, p, 0, keepdims=False) for p in place], 0)


def plane_scatter(v, chips, core, chip):
    bits = chips.bit_length() - 1
    for s in range(bits):
        masks = 1 << (bits - 1 - s), 1 << s
        mask = jnp.where(core == 0, *masks)
        bit = (chip & mask) // mask
        rows = v.shape[0] // 2
        half = lambda k: lax.dynamic_slice_in_dim(v, k * rows, rows, 0)
        pairs = [(i, i ^ (2 * masks[i % 2])) for i in range(2 * chips)]
        v = half(bit) + lax.ppermute(half(1 - bit), "gr", pairs)
    reverse = lambda k: sum(((k >> b) & 1) << (bits - 1 - b) for b in range(bits))
    return v, [(reverse(k), k) for k in range(chips)]


def on_device(x_states, y_states):
    rows, width = x_states.shape
    n = width // B
    gr, gc = lax.axis_size("gr"), lax.axis_size("gc")
    chips = gr // 2
    total_rows = rows * gr * gc
    core = lax.axis_index("gr") % 2
    chip = lax.axis_index("gr") // 2
    plane = lax.axis_index("gc")
    core_arg = jnp.reshape(core, (1,)).astype(jnp.int32)
    smem = pl.BlockSpec(memory_space=pltpu.SMEM)
    vmem = pl.BlockSpec(memory_space=pltpu.VMEM)
    hbm = pl.BlockSpec(memory_space=pltpu.HBM)
    folded = folded_rows(n)
    half = width * width // 2 // B
    panel = pltpu.VMEM((rows, width), BF)
    gram = pltpu.VMEM((folded, B), F32)
    extra = pltpu.VMEM((B, B), F32)
    packed = jax.ShapeDtypeStruct((folded + half + B, B), F32)

    other, own = pl.pallas_call(
        gram_kernel,
        out_shape=(packed,) * 2,
        in_specs=[smem, vmem, vmem],
        out_specs=(vmem,) * 2,
        scratch_shapes=[gram, extra] * 2,
        compiler_params=params(10),
        cost_estimate=pl.CostEstimate(flops=4 * rows * (folded + half) * B, bytes_accessed=8 * rows * width, transcendentals=0),
        name="gram",
    )(core_arg, x_states, y_states)
    sums = own + shift(other, "gr", 1)
    shards = chips * gc
    blocks = lambda v: jnp.reshape(v, (shards, -1, B))
    flat = lambda v: jnp.reshape(v, (-1, B))
    parts = sums[:folded], sums[folded + half :], sums[folded : folded + half]
    sums = flat(jnp.concatenate([blocks(v) for v in parts], 1))
    sums, place = plane_scatter(sums, chips, core, chip)
    place = [chip ^ jnp.where(core == 0, b, a) for a, b in place]
    sums = scatter_end(scatter_start(sums, "gc", gc, 1, plane))
    sums = gather_end(gather_start(sums, "gc", gc, 1), [plane ^ k for k in range(gc)])
    sums = jnp.reshape(sums, (gc, -1, B))
    size = (folded + B) // shards
    cov = gather_start(flat(sums[:, : size]), "gr", chips, 2)
    cxy = gather_start(flat(sums[:, size :]), "gr", chips, 2)
    cov = gather_end(cov, place)

    tri = B * len(lower_blocks(n))
    white = pl.pallas_call(
        lambda *refs: factor_kernel(float(total_rows), n, shards, *refs),
        out_shape=jax.ShapeDtypeStruct((tri, B), F32),
        in_specs=[vmem],
        out_specs=vmem,
        scratch_shapes=[pltpu.VMEM((width, width), F32)],
        compiler_params=params(8),
        cost_estimate=pl.CostEstimate(flops=20_000_000_000, bytes_accessed=8 * tri * B, transcendentals=0),
        name="factor",
    )(cov)
    cxy, white = lax.optimization_barrier((cxy, white))
    cxy = gather_end(cxy, place) / total_rows
    cxy_other = shift(cxy, "gr", 1)
    white_other = shift(white, "gr", 1)

    return pl.pallas_call(
        project_kernel,
        out_shape=(
            jax.ShapeDtypeStruct((rows, width), BF),
            jax.ShapeDtypeStruct((rows, width), BF),
            jax.ShapeDtypeStruct((width, width), F32),
        ),
        in_specs=[smem] + [vmem] * 6,
        out_specs=(hbm,) * 3,
        scratch_shapes=[panel] * 2 + [pltpu.VMEM((width, width), F32)] * 4 + [pltpu.SemaphoreType.DMA((1 + 2 * CHUNKS,))],
        compiler_params=params(24),
        cost_estimate=pl.CostEstimate(flops=8 * rows * width * width, bytes_accessed=16 * rows * width, transcendentals=0),
        name="project",
    )(core_arg, x_states, y_states, white, white_other, cxy, cxy_other)


def solution(mesh):
    return jax.shard_map(
        on_device,
        mesh=mesh,
        in_specs=(P(("gr", "gc"), None), P(("gr", "gc"), None)),
        out_specs=(P(("gr", "gc"), None), P(("gr", "gc"), None), P()),
        check_vma=False,
    )
```
